512 devices in a mesh: clip: 8 (over y, core), blk: 16 (over x, z_hi), uly: 4 (over z_lo).
Axes of the slice: x: 4, y: 4, z: 16 (z_hi: 4, z_lo: 4; z = z_hi * 4 + z_lo), core: 2. Of those that a mesh axis runs over, the one named last changes fastest.
Arguments:
- queries: bfloat16 [49152, 2560], P(('clip', 'blk', 'uly')), parts along dimension 0, may hold values from -8 to 8
- keys: bfloat16 [49152, 2560], P(('clip', 'blk', 'uly')), parts along dimension 0, may hold values from -8 to 8
- values: bfloat16 [49152, 2560], P(('clip', 'blk', 'uly')), parts along dimension 0, may hold values from -6 to 6
- text_keys: bfloat16 [4096, 2560], P('clip', 'uly'), parts along dimension 0, may hold values from -8 to 8
- text_values: bfloat16 [4096, 2560], P('clip', 'uly'), parts along dimension 0, may hold values from -6 to 6
- text_len: int32 [8], P('clip'), parts along dimension 0, may hold values from 128 to 512
- tile_map: int32 [128], P('clip'), parts along dimension 0, may hold values from 0 to 15, as said below
- mod_gain: float32 [2560], replicated, may hold values from 0.1 to 1.9
- mod_shift: float32 [2560], replicated, may hold values from -3 to 3
- head_weight: bfloat16 [2560, 64], replicated, may hold values from -0.125 to 0.125
- head_bias: float32 [64], replicated, may hold values from -3 to 3
- conv_weight: bfloat16 [432, 384], replicated, may hold values from -0.3125 to 0.3125
- conv_bias: float32 [384], replicated, may hold values from -3 to 3
- norm_gain: float32 [384], replicated, may hold values from 0.1 to 1.9
Outputs:
- video_features: bfloat16 [128, 32, 48, 384], P(('clip', 'blk'), 'uly'), parts along dimension 0
The draws below stay inside these ranges and needn't reach their ends.
There are 8 independent parts, one for each index of `clip`. The reference program is written for one: setup_inputs(seed, part) draws one part's arguments, and reference() takes and returns one part's arrays. A program takes and returns all parts, laid end to end along the dimension named above; an argument that names none is the same for every part. Nothing has to cross between parts.
Inputs may be any that keep to these rules, and one draw needn't show every extreme that they name: Text keys at index text_len or later are padding. A permutation: token block b, the tokens on index b of blk, holds latent frame tile_map[b].
All inputs are finite; a program needn't handle non-finite values.
Results may differ from the reference program's by a relative error of at most 0.012.
Values may be sent and summed in bfloat16 or wider, within the bound.
No kernel may reach another device: no remote copies, remote signals or barrier semaphores. Data moves between devices by JAX's collectives and lax.ppermute only.
A program may use at most 192 MiB of HBM per device.

```python
import jax
import jax.numpy as jnp
from jax import lax

PR_DEV = 4
PCOL = 24
HEADS = 20
HDIM = 128
TXT = 512
LAT = 16
C_OUT = 384
HD = 2560
TOKENS = 6144
FRAMES = 16
LH = 32
LW = 48
N_BLK = 16
N_ULY = 4


def draw_queries(key, part):
    key = jax.random.fold_in(key, 1)
    result = 1.5 * jax.random.truncated_normal(key, -5.0, 5.0, (TOKENS, HD), jnp.float32)
    return result.astype(jnp.bfloat16)


def draw_keys(key, part):
    key = jax.random.fold_in(key, 2)
    result = 1.5 * jax.random.truncated_normal(key, -5.0, 5.0, (TOKENS, HD), jnp.float32)
    return result.astype(jnp.bfloat16)


def draw_text_keys(key, part):
    key = jax.random.fold_in(key, 3)
    result = 1.5 * jax.random.truncated_normal(key, -5.0, 5.0, (TXT, HD), jnp.float32)
    return result.astype(jnp.bfloat16)


def draw_tile_map(key, part):
    key = jax.random.fold_in(key, 4)
    shuffled = jax.random.permutation(key, N_BLK).astype(jnp.int32)
    position = jnp.arange(N_BLK, dtype=jnp.int32)
    target = (jnp.asarray(part, jnp.int32) % N_BLK).astype(jnp.int32)
    where_target = jnp.sum(jnp.where(shuffled == target, position, 0)).astype(jnp.int32)
    first_value = shuffled[0]
    result = jnp.where(position == 0, target, jnp.where(position == where_target, first_value, shuffled))
    return result.astype(jnp.int32)


def shard_levels(rng, dims, split, low, largest):
    gain, own = 1.0, jax.random.fold_in(rng, 6)
    for dim, shards_of in split:
        draws = jnp.exp(jax.random.uniform(jax.random.fold_in(own, dim), (shards_of,), jnp.float32, low / len(split), largest / len(split)))
        gain = gain * jnp.repeat(draws, dims[dim] // shards_of).reshape([-1 if axis == dim else 1 for axis in range(len(dims))])
    return gain


def scatter_about(rng, extent, scale, limit, split=(), kind=jnp.bfloat16):
    gain = shard_levels(rng, extent, split, -0.22, 0.18) if split else 1.0
    array = jax.random.normal(rng, extent, jnp.float32) * scale * gain
    return jnp.minimum(jnp.maximum(array, -limit), limit).astype(kind)


def setup_inputs(seed: int = 0, part: int = 0) -> dict:
    streams_of = jax.random.split(jax.random.key(seed), 15)
    part_keys = jax.random.split(jax.random.fold_in(streams_of[14], part), 15)
    return {
        "queries": draw_queries(jax.random.fold_in(jax.random.fold_in(streams_of[14], part), 71), part),
        "keys": draw_keys(jax.random.fold_in(jax.random.fold_in(streams_of[14], part), 71), part),
        "values": scatter_about(part_keys[2], (TOKENS, HD), 1.0, 6.0, ((0, 64),)),
        "text_keys": draw_text_keys(jax.random.fold_in(jax.random.fold_in(streams_of[14], part), 71), part),
        "text_values": scatter_about(part_keys[4], (TXT, HD), 1.0, 6.0, ((1, 4),)),
        "text_len": jax.random.randint(part_keys[5], (1,), TXT // 4, TXT + 1).astype(jnp.int32),
        "tile_map": draw_tile_map(jax.random.fold_in(jax.random.fold_in(streams_of[14], part), 71), part),
        "mod_gain": jnp.clip(1.0 + 0.18 * jax.random.normal(streams_of[7], (HD,), jnp.float32), 0.1, 1.9),
        "mod_shift": scatter_about(streams_of[8], (HD,), 0.5, 3.0, (), jnp.float32),
        "head_weight": scatter_about(streams_of[9], (HD, 4 * LAT), HD ** -0.5, 0.125),
        "head_bias": scatter_about(streams_of[10], (4 * LAT,), 0.5, 3.0, (), jnp.float32),
        "conv_weight": scatter_about(streams_of[11], (27 * LAT, C_OUT), (27 * LAT) ** -0.5, 0.3125),
        "conv_bias": scatter_about(streams_of[12], (C_OUT,), 0.5, 3.0, (), jnp.float32),
        "norm_gain": jnp.clip(1.0 + 0.18 * jax.random.normal(streams_of[13], (C_OUT,), jnp.float32), 0.1, 1.9),
    }


def reference(queries, keys, values, text_keys, text_values, text_len, tile_map, mod_gain, mod_shift, head_weight, head_bias, conv_weight, conv_bias, norm_gain):
    scaling = HDIM ** (-0.5)
    usable = jnp.arange(TXT) < text_len[0]

    def split_heads(matrix, count):
        return matrix.reshape(count, HEADS, HDIM).transpose(1, 0, 2)

    def one_head(operands):
        query_head, key_head, value_head, text_key_head, text_value_head = operands
        scores = jnp.dot(query_head, key_head.T, preferred_element_type=jnp.float32) * scaling
        weights = jnp.exp(scores - lax.optimization_barrier(jnp.max(scores, axis=-1, keepdims=True)))
        total = lax.optimization_barrier(jnp.sum(weights, axis=-1, keepdims=True))
        self_out = jnp.dot(weights.astype(jnp.bfloat16), value_head, preferred_element_type=jnp.float32) / total
        text_scores = jnp.dot(query_head, text_key_head.T, preferred_element_type=jnp.float32) * scaling
        text_scores = jnp.where(usable[None, :], text_scores, -1e+30)
        text_weights = jnp.where(usable[None, :], jnp.exp(text_scores - lax.optimization_barrier(jnp.max(text_scores, axis=-1, keepdims=True))), 0.0)
        text_total = lax.optimization_barrier(jnp.sum(text_weights, axis=-1, keepdims=True))
        cross_out = jnp.dot(text_weights.astype(jnp.bfloat16), text_value_head, preferred_element_type=jnp.float32) / text_total
        return self_out + cross_out
    results = lax.map(one_head, (split_heads(queries, TOKENS), split_heads(keys, TOKENS), split_heads(values, TOKENS), split_heads(text_keys, TXT), split_heads(text_values, TXT)))
    attended = results.transpose(1, 0, 2).reshape(TOKENS, HD).astype(jnp.bfloat16)
    features = attended.astype(jnp.float32)
    average = lax.optimization_barrier(jnp.mean(features, axis=-1, keepdims=True))
    variance = lax.optimization_barrier(jnp.mean((features - average) ** 2, axis=-1, keepdims=True))
    normed = ((features - average) * lax.rsqrt(variance + 1e-06) * mod_gain + mod_shift).astype(jnp.bfloat16)
    patches = (jnp.dot(normed, head_weight, preferred_element_type=jnp.float32) + head_bias).astype(jnp.bfloat16)
    blocks = patches.reshape(N_BLK, N_ULY, PR_DEV, PCOL, 2, 2, LAT).transpose(0, 1, 2, 4, 3, 5, 6).reshape(N_BLK, LH, LW, LAT)
    latent = jnp.zeros_like(blocks).at[tile_map].set(blocks)
    padded = jnp.pad(latent, ((2, 0), (1, 1), (1, 1), (0, 0)))
    stacked_taps = []
    for frame_tap in range(3):
        for row_tap in range(3):
            for col_tap in range(3):
                stacked_taps.append(padded[frame_tap:frame_tap + FRAMES, row_tap:row_tap + LH, col_tap:col_tap + LW])
    stacked = jnp.concatenate(stacked_taps, axis=-1).reshape(FRAMES * LH * LW, 27 * LAT)
    pre = jnp.dot(stacked, conv_weight, preferred_element_type=jnp.float32) + conv_bias
    normalized = pre * lax.rsqrt(lax.optimization_barrier(jnp.mean(pre * pre, axis=-1, keepdims=True)) + 1e-06) * norm_gain
    return jax.nn.silu(normalized).astype(jnp.bfloat16).reshape(FRAMES, LH, LW, C_OUT)
```

```python
import functools

import jax
import jax.numpy as jnp
from jax import lax
from jax.experimental import pallas as pl
from jax.experimental.pallas import tpu as pltpu
from jax.sharding import Mesh, PartitionSpec as P

PCOL = 24
HDIM = 128
TXT = 512
LAT = 16
ROWS = 96
NZ = 16
C_OUT = 384
LOG2E = 1.4426950408889634
SCALE2 = HDIM ** (-0.5) * LOG2E
Z = ("zh", "zl")
F32 = jnp.float32
BF = jnp.bfloat16
VMEM_LIMIT = 50 * 1024 * 1024


def params():
    return pltpu.CompilerParams(vmem_limit_bytes=VMEM_LIMIT)


def vmem():
    return pl.BlockSpec(memory_space=pltpu.VMEM)


def smem():
    return pl.BlockSpec(memory_space=pltpu.SMEM)


def pack_kernel(q_ref, k_ref, v_ref, kvm_ref, kve_ref, q_out):
    for zl in range(4):
        last = (5 * zl + 4) * HDIM
        queries_last = q_ref[:, last : last + HDIM].astype(F32)
        for zh in range(4):
            z = zh * 4 + zl
            lo = (5 * zl + zh) * HDIM
            kvm_ref[z, 0:ROWS, :] = k_ref[:, lo : lo + HDIM]
            kvm_ref[z, ROWS : 2 * ROWS, :] = v_ref[:, lo : lo + HDIM]
            kve_ref[z, 0:ROWS, :] = k_ref[:, last : last + HDIM]
            kve_ref[z, ROWS : 2 * ROWS, :] = v_ref[:, last : last + HDIM]
            q_out[z, 0:ROWS, :] = q_ref[:, lo : lo + HDIM]
            part = queries_last[24 * zh : 24 * zh + 24]
            q_out[z, ROWS : ROWS + 32, :] = jnp.concatenate(
                [part, jnp.zeros((8, HDIM), F32)], axis=0
            ).astype(BF)


def pack(queries, keys, values):
    return pl.pallas_call(
        pack_kernel,
        out_shape=(
            jax.ShapeDtypeStruct((NZ, 2 * ROWS, HDIM), BF),
            jax.ShapeDtypeStruct((NZ, 2 * ROWS, HDIM), BF),
            jax.ShapeDtypeStruct((NZ, ROWS + 32, HDIM), BF),
        ),
        in_specs=[vmem()] * 3,
        out_specs=(vmem(),) * 3,
        compiler_params=params(),
    )(queries, keys, values)


def dot_t(a, b):
    return lax.dot_general(a, b, (((1,), (1,)), ((), ())), preferred_element_type=F32)


def attend(query, pieces, text_key, text_value, text_len, scores_ref):
    rows = query.shape[0]
    top = None
    at = 0
    spans = []
    for ref, lo, hi in pieces:
        key = ref[lo:hi, 0:ROWS, :].reshape((hi - lo) * ROWS, HDIM)
        scores = dot_t(query, key)
        width = scores.shape[1]
        scores_ref[:, at : at + width] = scores
        for col in range(0, width, HDIM):
            part = scores[:, col : col + HDIM]
            top = part if top is None else jnp.maximum(top, part)
        spans.append((at, width))
        at += width
    peak = jnp.max(top, axis=-1, keepdims=True) * SCALE2
    total = jnp.zeros((rows, 2 * HDIM), F32)
    for (ref, lo, hi), (start, width) in zip(pieces, spans):
        weights = jnp.exp2(scores_ref[:, start : start + width] * SCALE2 - peak).astype(BF)
        value = ref[lo:hi, ROWS : 2 * ROWS, :].reshape(width, HDIM)
        wide = jnp.concatenate([value, jnp.ones((width, HDIM), BF)], axis=1)
        total = total + jnp.dot(weights, wide, preferred_element_type=F32)
    self_out = total[:, :HDIM] / total[:, HDIM:]
    text_scores = dot_t(query, text_key) * SCALE2
    usable = lax.broadcasted_iota(jnp.int32, text_scores.shape, 1) < text_len
    text_scores = jnp.where(usable, text_scores, -1e30)
    text_peak = jnp.max(text_scores, axis=-1, keepdims=True)
    text_weights = jnp.where(usable, jnp.exp2(text_scores - text_peak), 0.0).astype(BF)
    wide = jnp.concatenate([text_value, jnp.ones((TXT, HDIM), BF)], axis=1)
    text_total = jnp.dot(text_weights, wide, preferred_element_type=F32)
    return self_out + text_total[:, :HDIM] / text_total[:, HDIM:]


def pieces_of(refs):
    pieces = []
    for ref in refs:
        count = ref.shape[0]
        for lo in range(0, count, 8):
            pieces.append((ref, lo, lo + 8))
    return pieces


def main_kernel(info, q_ref, k0, k1, k2, k3, k4, tk_ref, tv_ref, out_ref, scores_ref):
    query = q_ref[:, 0:ROWS, :].reshape(4 * ROWS, HDIM)
    column = pl.ds(pl.multiple_of(info[0] * HDIM, HDIM), HDIM)
    result = attend(
        query,
        pieces_of((k0, k1, k2, k3, k4)),
        tk_ref[:, column],
        tv_ref[:, column],
        info[1],
        scores_ref,
    )
    out_ref[...] = result.astype(BF).reshape(4, ROWS, HDIM)


def extra_kernel(info, q_ref, k0, k1, k2, k3, k4, tk_ref, tv_ref, main_ref, out_ref, scores_ref):
    query = q_ref[:, ROWS : ROWS + 32, :].astype(F32)[:, :24].reshape(NZ * 24, HDIM).astype(BF)
    column = slice(4 * HDIM, 5 * HDIM)
    result = attend(
        query,
        pieces_of((k0, k1, k2, k3, k4)),
        tk_ref[:, column],
        tv_ref[:, column],
        info[1],
        scores_ref,
    )
    padded = jnp.concatenate(
        [result.reshape(NZ, 24, HDIM), jnp.zeros((NZ, 8, HDIM), F32)], axis=1
    )
    out_ref[:, 0:ROWS, :] = main_ref[...]
    out_ref[:, ROWS : ROWS + 32, :] = padded.astype(BF)


KEYS = 6144


def cost(rows):
    return pl.CostEstimate(
        flops=rows * (KEYS + TXT) * HDIM * 8,
        bytes_accessed=2 * KEYS * HDIM * 2,
        transcendentals=rows * (KEYS + TXT),
    )


def main_attention(info, q_all, kv, text_keys, text_values):
    whole = lambda a: pl.BlockSpec(a.shape, lambda i, n=a.ndim: (0,) * n)
    return pl.pallas_call(
        main_kernel,
        grid=(4,),
        out_shape=jax.ShapeDtypeStruct((NZ, ROWS, HDIM), BF),
        in_specs=[smem(), pl.BlockSpec((4, ROWS + 32, HDIM), lambda i: (i, 0, 0))]
        + [whole(a) for a in kv]
        + [whole(text_keys), whole(text_values)],
        out_specs=pl.BlockSpec((4, ROWS, HDIM), lambda i: (i, 0, 0)),
        scratch_shapes=[pltpu.VMEM((4 * ROWS, KEYS), F32)],
        compiler_params=params(),
        cost_estimate=cost(1536),
    )(info, q_all, *kv, text_keys, text_values)


def extra_attention(info, q_all, kv, text_keys, text_values, main_out):
    return pl.pallas_call(
        extra_kernel,
        out_shape=jax.ShapeDtypeStruct((NZ, ROWS + 32, HDIM), BF),
        in_specs=[smem()] + [vmem()] * 9,
        out_specs=vmem(),
        scratch_shapes=[pltpu.VMEM((NZ * 24, KEYS), F32)],
        compiler_params=params(),
        cost_estimate=cost(384),
    )(info, q_all, *kv, text_keys, text_values, main_out)


def head_kernel(back_ref, gain_ref, shift_ref, weight_ref, bias_ref, out_ref):
    blocks = []
    for head in range(20):
        zl, zh = head // 5, head % 5
        if zh < 4:
            blocks.append(back_ref[zh * 4 + zl, 0:ROWS, :].astype(F32))
        else:
            blocks.append(
                jnp.concatenate(
                    [
                        back_ref[part * 4 + zl, ROWS : ROWS + 32, :].astype(F32)[:24]
                        for part in range(4)
                    ],
                    axis=0,
                )
            )
    count = 20 * HDIM
    average = jnp.sum(sum(blocks), axis=-1, keepdims=True) / count
    blocks = [block - average for block in blocks]
    variance = jnp.sum(sum(block * block for block in blocks), axis=-1, keepdims=True) / count
    scale = lax.rsqrt(variance + 1e-06)
    patches = jnp.zeros((ROWS, 64), F32)
    for head in range(20):
        span = slice(head * HDIM, (head + 1) * HDIM)
        normed = (blocks[head] * scale * gain_ref[:, span] + shift_ref[:, span]).astype(BF)
        patches = patches + jnp.dot(normed, weight_ref[span, :], preferred_element_type=F32)
    out_ref[...] = (patches + bias_ref[...]).astype(BF)


def head(back, mod_gain, mod_shift, head_weight, head_bias):
    return pl.pallas_call(
        head_kernel,
        out_shape=jax.ShapeDtypeStruct((ROWS, 64), BF),
        in_specs=[vmem()] * 5,
        out_specs=vmem(),
        compiler_params=params(),
    )(back, mod_gain[None], mod_shift[None], head_weight, head_bias[None])


def conv_kernel(
    info, tile_map, g0, g1, g2, g3, weight_ref, bias_ref, gain_ref, out_ref, wide_ref, slab_ref, pix_ref
):
    wide_ref[...] = jnp.zeros_like(wide_ref)
    for a in range(3):
        for di in (-1, 0, 1):
            for dj in (-1, 0, 1):
                for p in range(2):
                    for q in range(2):
                        row = ((dj + 1) * 4 + p * 2 + q) * LAT
                        for pp in range(2):
                            for qq in range(2):
                                r = 2 * di + p - pp + 1
                                s = 2 * dj + q - qq + 1
                                if 0 <= r < 3 and 0 <= s < 3:
                                    tap = ((a * 3 + r) * 3 + s) * LAT
                                    col = (pp * 2 + qq) * C_OUT
                                    wide_ref[
                                        a * 3 + di + 1, row : row + LAT, col : col + C_OUT
                                    ] = weight_ref[tap : tap + LAT, :]
    for d, ref in enumerate((g0, g1, g2, g3)):
        slab_ref[4 * d : 4 * d + 4] = ref[...]
    x, zh = info[2], info[0]
    pre = jnp.zeros((ROWS, 4 * C_OUT), F32)
    column = lax.broadcasted_iota(jnp.int32, (6 * PCOL, 64), 0) % PCOL
    for a in range(3):
        wanted = 4 * x + zh - 2 + a
        source = jnp.int32(0)
        for b in range(16):
            source = jnp.where(tile_map[b] == wanted, b, source)
        place = lax.rem(x - source // 4 + 4, 4) * 4 + lax.rem(zh - lax.rem(source, 4) + 4, 4)
        slab = slab_ref[place].astype(F32)
        slab = jnp.where(wanted >= 0, slab, 0.0)
        zero = jnp.zeros((8, 64), F32)
        tall = jnp.concatenate([zero, slab, zero], axis=0)
        left = jnp.where(column == 0, 0.0, tall[7 : 7 + 6 * PCOL])
        right = jnp.where(column == PCOL - 1, 0.0, tall[9 : 9 + 6 * PCOL])
        joined = jnp.concatenate([left, slab, right], axis=1)
        for di in range(3):
            part = joined[di * PCOL : di * PCOL + ROWS].astype(BF)
            pre = pre + jnp.dot(part, wide_ref[a * 3 + di], preferred_element_type=F32)
    for pp in range(2):
        for qq in range(2):
            at = (pp * 2 + qq) * C_OUT
            value = pre[:, at : at + C_OUT] + bias_ref[...]
            mean = jnp.mean(value * value, axis=-1, keepdims=True)
            value = value * lax.rsqrt(mean + 1e-06) * gain_ref[...]
            value = value / (1.0 + jnp.exp(-value))
            for i in range(4):
                for part in range(3):
                    pix_ref[part, 2 * i + pp, pl.ds(qq, PCOL, 2), :] = value[
                        i * PCOL : (i + 1) * PCOL, part * HDIM : (part + 1) * HDIM
                    ]
    for part in range(3):
        out_ref[:, :, part * HDIM : (part + 1) * HDIM] = pix_ref[part].astype(BF)


def conv(info, tile_map, gathered, conv_weight, conv_bias, norm_gain):
    return pl.pallas_call(
        conv_kernel,
        out_shape=jax.ShapeDtypeStruct((8, 48, C_OUT), BF),
        in_specs=[smem(), smem()] + [vmem()] * 7,
        out_specs=vmem(),
        scratch_shapes=[
            pltpu.VMEM((9, 192, 4 * C_OUT), BF),
            pltpu.VMEM((16, 6 * PCOL, 64), BF),
            pltpu.VMEM((3, 8, 48, HDIM), F32),
        ],
        compiler_params=params(),
    )(info, tile_map, *gathered, conv_weight, conv_bias[None], norm_gain[None])


def shift(block, axis, distance):
    return lax.ppermute(block, axis, [(i, (i + distance) % 4) for i in range(4)])


def around_x(block):
    right = shift(block, "x", 1)
    left = shift(block, "x", -1)
    half = block.shape[0] // 2
    return (block, right, left, shift(right[:half], "x", 1), shift(left[half:], "x", -1))


def per_device(
    queries,
    keys,
    values,
    text_keys,
    text_values,
    text_len,
    tile_map,
    mod_gain,
    mod_shift,
    head_weight,
    head_bias,
    conv_weight,
    conv_bias,
    norm_gain,
):
    exchange = functools.partial(
        lax.all_to_all, axis_name=Z, split_axis=0, concat_axis=0, tiled=True
    )
    x, zh = lax.axis_index("x"), lax.axis_index("zh")
    info = jnp.stack([zh, text_len[0], x]).astype(jnp.int32)
    main_send, extra_send, q_send = pack(queries, keys, values)
    main_kv = around_x(exchange(main_send))
    extra_kv = around_x(exchange(extra_send))
    q_all = exchange(q_send)
    main_out = main_attention(info, q_all, main_kv, text_keys, text_values)
    out = extra_attention(info, q_all, extra_kv, text_keys, text_values, main_out)
    back = exchange(out)
    patches = head(back, mod_gain, mod_shift, head_weight, head_bias)
    above = lax.ppermute(patches[ROWS - PCOL :], "zl", [(i, i + 1) for i in range(3)])
    below = lax.ppermute(patches[:PCOL], "zl", [(i + 1, i) for i in range(3)])
    slab = jnp.concatenate([above, patches, below], axis=0)
    line = jnp.stack([slab] + [shift(slab, "zh", d) for d in (1, 2, 3)])
    gathered = [line] + [shift(line, "x", d) for d in (1, 2, 3)]
    out = conv(info, tile_map, gathered, conv_weight, conv_bias, norm_gain)
    return out[None]


def solution(mesh):
    inner = Mesh(mesh.devices.reshape(8, 4, 4, 4), ("clip", "x", "zh", "zl"))
    tokens = P(("clip", "x", "zh", "zl"), None)
    placed = (
        tokens,
        tokens,
        tokens,
        P("clip", "zl"),
        P("clip", "zl"),
        P("clip"),
        P("clip"),
    ) + (P(),) * 7
    return jax.shard_map(
        per_device,
        mesh=inner,
        in_specs=placed,
        out_specs=P(("clip", "x", "zh"), "zl", None, None),
        check_vma=False,
    )
```

```python
import functools

import jax
import jax.numpy as jnp
from jax import lax
from jax.experimental import pallas as pl
from jax.experimental.pallas import tpu as pltpu
from jax.sharding import Mesh, PartitionSpec as P

PCOL = 24
HDIM = 128
TXT = 512
LAT = 16
ROWS = 96
NZ = 16
C_OUT = 384
LOG2E = 1.4426950408889634
SCALE2 = HDIM ** (-0.5) * LOG2E
Z = ("zh", "zl")
F32 = jnp.float32
BF = jnp.bfloat16
VMEM_LIMIT = 50 * 1024 * 1024


def params():
    return pltpu.CompilerParams(vmem_limit_bytes=VMEM_LIMIT)


def vmem():
    return pl.BlockSpec(memory_space=pltpu.VMEM)


def smem():
    return pl.BlockSpec(memory_space=pltpu.SMEM)


PART = 24
SLOT = 32


def pack_kernel(q_ref, k_ref, v_ref, shared_out, kv_out, q_out):
    for zl in range(4):
        last = slice((5 * zl + 4) * HDIM, (5 * zl + 5) * HDIM)
        queries_last = q_ref[:, last].astype(F32)
        for zh in range(4):
            z = zh * 4 + zl
            own = slice((5 * zl + zh) * HDIM, (5 * zl + zh + 1) * HDIM)
            shared_out[z, 0:ROWS, :] = k_ref[:, last]
            shared_out[z, ROWS : 2 * ROWS, :] = v_ref[:, last]
            part = queries_last[PART * zh : PART * (zh + 1)]
            shared_out[z, 2 * ROWS : 2 * ROWS + SLOT, :] = jnp.concatenate(
                [part, jnp.zeros((SLOT - PART, HDIM), F32)], axis=0
            ).astype(BF)
            kv_out[z, 0:ROWS, :] = k_ref[:, own]
            kv_out[z, ROWS : 2 * ROWS, :] = v_ref[:, own]
            q_out[z] = q_ref[:, own]


def pack(queries, keys, values):
    return pl.pallas_call(
        pack_kernel,
        out_shape=(
            jax.ShapeDtypeStruct((NZ, 2 * ROWS + SLOT, HDIM), BF),
            jax.ShapeDtypeStruct((NZ, 2 * ROWS, HDIM), BF),
            jax.ShapeDtypeStruct((NZ, ROWS, HDIM), BF),
        ),
        in_specs=[vmem()] * 3,
        out_specs=(vmem(),) * 3,
        compiler_params=params(),
    )(queries, keys, values)


def dot_t(a, b):
    return lax.dot_general(a, b, (((1,), (1,)), ((), ())), preferred_element_type=F32)


def attend(query, pieces, text_key, text_value, text_len):
    ones = jnp.ones((HDIM, HDIM), BF)

    def scores_of(piece):
        ref, lo, hi = piece
        return dot_t(query, ref[lo:hi, 0:ROWS, :].reshape((hi - lo) * ROWS, HDIM))

    def row_peak(scores):
        top = scores[:, :HDIM]
        for col in range(HDIM, scores.shape[1], HDIM):
            top = jnp.maximum(top, scores[:, col : col + HDIM])
        return jnp.max(top, axis=-1, keepdims=True)

    def widened(value):
        return jnp.concatenate([value, jnp.tile(ones, (value.shape[0] // HDIM, 1))], axis=1)

    peak, total = None, None
    scores = scores_of(pieces[0])
    for index, (ref, lo, hi) in enumerate(pieces):
        later = scores_of(pieces[index + 1]) if index + 1 < len(pieces) else None
        highest = row_peak(scores) * SCALE2
        value = widened(ref[lo:hi, ROWS : 2 * ROWS, :].reshape((hi - lo) * ROWS, HDIM))
        newest = highest if peak is None else jnp.maximum(peak, highest)
        weights = jnp.exp2(scores * SCALE2 - newest).astype(BF)
        part = jnp.dot(weights, value, preferred_element_type=F32)
        total = part if peak is None else total * jnp.exp2(peak - newest) + part
        peak, scores = newest, later
    self_out = total[:, :HDIM] / total[:, HDIM:]
    text_scores = dot_t(query, text_key) * SCALE2
    usable = lax.broadcasted_iota(jnp.int32, text_scores.shape, 1) < text_len
    text_scores = jnp.where(usable, text_scores, -1e30)
    text_peak = row_peak(text_scores)
    text_weights = jnp.where(usable, jnp.exp2(text_scores - text_peak), 0.0).astype(BF)
    text_total = jnp.dot(text_weights, widened(text_value), preferred_element_type=F32)
    return self_out + text_total[:, :HDIM] / text_total[:, HDIM:]


def pieces_of(refs):
    pieces = []
    for ref in refs:
        count = ref.shape[0]
        for lo in range(0, count, 8):
            pieces.append((ref, lo, min(lo + 8, count)))
    return pieces


def main_kernel(info, q_ref, k0, k1, k2, k3, k4, tk_ref, tv_ref, out_ref):
    query = q_ref[:, 0:ROWS, :].reshape(4 * ROWS, HDIM)
    column = pl.ds(pl.multiple_of(info[0] * HDIM, HDIM), HDIM)
    pieces = pieces_of((k0, k1, k2, k3, k4))
    result = attend(query, pieces, tk_ref[:, column], tv_ref[:, column], info[1])
    out_ref[...] = result.astype(BF).reshape(4, ROWS, HDIM)


def shared_kernel(info, s_ref, k1, k2, k3, k4, tk_ref, tv_ref, q_ref, out_ref):
    query = s_ref[:, 2 * ROWS : 2 * ROWS + SLOT, :].astype(F32)[:, :PART]
    query = query.reshape(NZ * PART, HDIM).astype(BF)
    column = slice(4 * HDIM, 5 * HDIM)
    pieces = pieces_of((s_ref, k1, k2, k3, k4))
    result = attend(query, pieces, tk_ref[:, column], tv_ref[:, column], info[1])
    filler = jnp.zeros((NZ, SLOT - PART, HDIM), F32)
    result = jnp.concatenate([result.reshape(NZ, PART, HDIM), filler], axis=1)
    out_ref[:, 0:ROWS, :] = q_ref[...]
    out_ref[:, ROWS : ROWS + SLOT, :] = result.astype(BF)


KEYS = 6144


def cost(rows):
    return pl.CostEstimate(
        flops=rows * (KEYS + TXT) * HDIM * 8,
        bytes_accessed=2 * KEYS * HDIM * 2,
        transcendentals=rows * (KEYS + TXT),
    )


def main_attention(info, queries, kv, text_keys, text_values):
    whole = lambda a: pl.BlockSpec(a.shape, lambda i, n=a.ndim: (0,) * n)
    return pl.pallas_call(
        main_kernel,
        grid=(NZ // 4,),
        out_shape=jax.ShapeDtypeStruct((NZ, ROWS, HDIM), BF),
        in_specs=[smem(), pl.BlockSpec((4,) + queries.shape[1:], lambda i: (i, 0, 0))]
        + [whole(a) for a in kv]
        + [whole(text_keys), whole(text_values)],
        out_specs=pl.BlockSpec((4, ROWS, HDIM), lambda i: (i, 0, 0)),
        compiler_params=params(),
        cost_estimate=cost(NZ * ROWS),
    )(info, queries, *kv, text_keys, text_values)


def shared_attention(info, kv, text_keys, text_values, queries):
    return pl.pallas_call(
        shared_kernel,
        out_shape=jax.ShapeDtypeStruct((NZ, ROWS + SLOT, HDIM), BF),
        in_specs=[smem()] + [vmem()] * 8,
        out_specs=vmem(),
        compiler_params=params(),
        cost_estimate=cost(NZ * PART),
    )(info, *kv, text_keys, text_values, queries)


def head_kernel(
    back_ref, shared_ref, gain_ref, shift_ref, weight_ref, bias_ref, out_ref
):
    blocks = []
    for head in range(20):
        zl, zh = head // 5, head % 5
        if zh < 4:
            block = back_ref[zh * 4 + zl].astype(F32)
        else:
            parts = [
                shared_ref[part * 4 + zl, ROWS : ROWS + SLOT, :].astype(F32)[:PART]
                for part in range(4)
            ]
            block = jnp.concatenate(parts, axis=0)
        blocks.append(block)
    count = 20 * HDIM
    average = jnp.sum(sum(blocks), axis=-1, keepdims=True) / count
    blocks = [block - average for block in blocks]
    variance = jnp.sum(sum(block * block for block in blocks), axis=-1, keepdims=True) / count
    scale = lax.rsqrt(variance + 1e-06)
    patches = jnp.zeros((ROWS, 64), F32)
    for head in range(20):
        span = slice(head * HDIM, (head + 1) * HDIM)
        normed = (blocks[head] * scale * gain_ref[:, span] + shift_ref[:, span]).astype(BF)
        patches = patches + jnp.dot(normed, weight_ref[span, :], preferred_element_type=F32)
    patches = patches + bias_ref[...]
    packed = jnp.concatenate([patches[: ROWS // 2], patches[ROWS // 2 :]], axis=1).astype(BF)
    for copy in range(NZ):
        out_ref[copy] = packed


def head(back, shared, mod_gain, mod_shift, head_weight, head_bias):
    return pl.pallas_call(
        head_kernel,
        out_shape=jax.ShapeDtypeStruct((NZ, ROWS // 2, HDIM), BF),
        in_specs=[vmem()] * 6,
        out_specs=vmem(),
        compiler_params=params(),
    )(back, shared, mod_gain[None], mod_shift[None], head_weight, head_bias[None])


SLAB = 72


def slab_kernel(info, line_ref, out_ref):
    zl = info[3]
    for zh in range(4):
        own = line_ref[zh * 4 + zl].astype(F32)
        above = line_ref[zh * 4 + jnp.maximum(zl - 1, 0)].astype(F32)[PCOL:, 64:]
        below = line_ref[zh * 4 + jnp.minimum(zl + 1, 3)].astype(F32)[:PCOL, :64]
        above = jnp.where(zl > 0, above, 0.0)
        below = jnp.where(zl < 3, below, 0.0)
        left = jnp.concatenate([above, own[:, :64]], axis=0)
        right = jnp.concatenate([own[:, 64:], below], axis=0)
        packed = jnp.concatenate([left, right], axis=1).astype(BF)
        for copy in range(4):
            out_ref[copy, zh] = packed


def slab_of(info, line):
    return pl.pallas_call(
        slab_kernel,
        out_shape=jax.ShapeDtypeStruct((4, 4, SLAB, HDIM), BF),
        in_specs=[smem(), vmem()],
        out_specs=vmem(),
        compiler_params=params(),
    )(info, line)


def conv_kernel(
    info, tile_map, slab_ref, weight_ref, bias_ref, gain_ref, out_ref, wide_ref, pix_ref
):
    wide_ref[...] = jnp.zeros_like(wide_ref)
    for a in range(3):
        for di in (-1, 0, 1):
            for dj in (-1, 0, 1):
                for p in range(2):
                    for q in range(2):
                        row = ((dj + 1) * 4 + p * 2 + q) * LAT
                        for pp in range(2):
                            for qq in range(2):
                                r = 2 * di + p - pp + 1
                                s = 2 * dj + q - qq + 1
                                if 0 <= r < 3 and 0 <= s < 3:
                                    tap = ((a * 3 + r) * 3 + s) * LAT
                                    col = (pp * 2 + qq) * C_OUT
                                    wide_ref[
                                        a * 3 + di + 1, row : row + LAT, col : col + C_OUT
                                    ] = weight_ref[tap : tap + LAT, :]
    x, zh = info[2], info[0]
    pre = jnp.zeros((ROWS, 4 * C_OUT), F32)
    column = lax.broadcasted_iota(jnp.int32, (6 * PCOL, 64), 0) % PCOL
    for a in range(3):
        wanted = 4 * x + zh - 2 + a
        source = jnp.int32(0)
        for b in range(16):
            source = jnp.where(tile_map[b] == wanted, b, source)
        slab = slab_ref[source].astype(F32)
        slab = jnp.concatenate([slab[:, :64], slab[:, 64:]], axis=0)
        slab = jnp.where(wanted >= 0, slab, 0.0)
        zero = jnp.zeros((8, 64), F32)
        tall = jnp.concatenate([zero, slab, zero], axis=0)
        left = jnp.where(column == 0, 0.0, tall[7 : 7 + 6 * PCOL])
        right = jnp.where(column == PCOL - 1, 0.0, tall[9 : 9 + 6 * PCOL])
        joined = jnp.concatenate([left, slab, right], axis=1)
        for di in range(3):
            part = joined[di * PCOL : di * PCOL + ROWS].astype(BF)
            pre = pre + jnp.dot(part, wide_ref[a * 3 + di], preferred_element_type=F32)
    for pp in range(2):
        for qq in range(2):
            at = (pp * 2 + qq) * C_OUT
            value = pre[:, at : at + C_OUT] + bias_ref[...]
            mean = jnp.mean(value * value, axis=-1, keepdims=True)
            value = value * lax.rsqrt(mean + 1e-06) * gain_ref[...]
            value = value / (1.0 + jnp.exp(-value))
            for i in range(4):
                for part in range(3):
                    pix_ref[part, 2 * i + pp, pl.ds(qq, PCOL, 2), :] = value[
                        i * PCOL : (i + 1) * PCOL, part * HDIM : (part + 1) * HDIM
                    ]
    for part in range(3):
        out_ref[:, :, part * HDIM : (part + 1) * HDIM] = pix_ref[part].astype(BF)


def conv(info, tile_map, gathered, conv_weight, conv_bias, norm_gain):
    return pl.pallas_call(
        conv_kernel,
        out_shape=jax.ShapeDtypeStruct((8, 48, C_OUT), BF),
        in_specs=[smem(), smem()] + [vmem()] * 4,
        out_specs=vmem(),
        scratch_shapes=[
            pltpu.VMEM((9, 192, 4 * C_OUT), BF),
            pltpu.VMEM((3, 8, 48, HDIM), F32),
        ],
        compiler_params=params(),
    )(info, tile_map, gathered, conv_weight, conv_bias[None], norm_gain[None])


def shift(block, axis, distance):
    return lax.ppermute(block, axis, [(i, (i + distance) % 4) for i in range(4)])


def around(block, axis):
    right = shift(block, axis, 1)
    left = shift(block, axis, -1)
    half = block.shape[0] // 2
    return (block, right, left, shift(right[:half], axis, 1), shift(left[half:], axis, -1))


def exchange(block, axis):
    return lax.all_to_all(block, axis, split_axis=0, concat_axis=0, tiled=True)


def per_device(
    queries,
    keys,
    values,
    text_keys,
    text_values,
    text_len,
    tile_map,
    mod_gain,
    mod_shift,
    head_weight,
    head_bias,
    conv_weight,
    conv_bias,
    norm_gain,
):
    x, zh, zl = (lax.axis_index(axis) for axis in ("x", "zh", "zl"))
    info = jnp.stack([zh, text_len[0], x, zl]).astype(jnp.int32)
    shared_send, kv_send, q_send = pack(queries, keys, values)
    shared = exchange(shared_send, Z)
    shared, kv_send = lax.optimization_barrier((shared, kv_send))
    shared_kv = (shared,) + around(shared[:, : 2 * ROWS], "x")[1:]
    kv = exchange(kv_send, Z)
    third_send = shared_attention(info, shared_kv, text_keys, text_values, q_send)
    kv, third_send = lax.optimization_barrier((kv, third_send))
    main_kv = around(kv, "x")
    third = exchange(third_send, Z)
    back = exchange(main_attention(info, third, main_kv, text_keys, text_values), Z)
    line = exchange(head(back, third, mod_gain, mod_shift, head_weight, head_bias), Z)
    plane = exchange(slab_of(info, line), "x")
    gathered = plane.reshape(16, SLAB, HDIM)
    out = conv(info, tile_map, gathered, conv_weight, conv_bias, norm_gain)
    return out[None]


def solution(mesh):
    inner = Mesh(mesh.devices.reshape(8, 4, 4, 4), ("clip", "x", "zh", "zl"))
    tokens = P(("clip", "x", "zh", "zl"), None)
    placed = (
        tokens,
        tokens,
        tokens,
        P("clip", "zl"),
        P("clip", "zl"),
        P("clip"),
        P("clip"),
    ) + (P(),) * 7
    return jax.shard_map(
        per_device,
        mesh=inner,
        in_specs=placed,
        out_specs=P(("clip", "x", "zh"), "zl", None, None),
        check_vma=False,
    )
```

```python
import functools

import jax
import jax.numpy as jnp
from jax import lax
from jax.experimental import pallas as pl
from jax.experimental.pallas import tpu as pltpu
from jax.sharding import Mesh, PartitionSpec as P

PCOL = 24
HDIM = 128
TXT = 512
LAT = 16
ROWS = 96
NZ = 16
C_OUT = 384
LOG2E = 1.4426950408889634
SCALE2 = HDIM ** (-0.5) * LOG2E
Z = ("zh", "zl")
F32 = jnp.float32
BF = jnp.bfloat16
VMEM_LIMIT = 50 * 1024 * 1024


def params():
    return pltpu.CompilerParams(vmem_limit_bytes=VMEM_LIMIT)


def vmem():
    return pl.BlockSpec(memory_space=pltpu.VMEM)


def smem():
    return pl.BlockSpec(memory_space=pltpu.SMEM)


PART = 24
SLOT = 32


def load_kernel(q_hbm, k_hbm, v_hbm, main_out, kv_out, q_out, q_ref, k_ref, v_ref, sems):
    width = 5 * HDIM
    copies = []
    for zl in range(4):
        span = slice(zl * width, (zl + 1) * width)
        for index, (source, target) in enumerate(((k_hbm, k_ref), (v_hbm, v_ref), (q_hbm, q_ref))):
            copy = pltpu.make_async_copy(
                source.at[:, span], target.at[:, span], sems.at[3 * zl + index]
            )
            copy.start()
            copies.append(copy)
    for zl in range(4):
        for copy in copies[3 * zl : 3 * zl + 3]:
            copy.wait()
        last = slice((5 * zl + 4) * HDIM, (5 * zl + 5) * HDIM)
        q_out[zl] = q_ref[:, last]
        kv_out[zl, 0:ROWS, :] = k_ref[:, last]
        kv_out[zl, ROWS : 2 * ROWS, :] = v_ref[:, last]
        for index, ref in enumerate((k_ref, v_ref, q_ref)):
            rows = slice(index * ROWS, (index + 1) * ROWS)
            for zh in range(4):
                own = slice((5 * zl + zh) * HDIM, (5 * zl + zh + 1) * HDIM)
                main_out[zh * 4 + zl, rows, :] = ref[:, own]


def load(queries, keys, values):
    return pl.pallas_call(
        load_kernel,
        out_shape=(
            jax.ShapeDtypeStruct((NZ, 3 * ROWS, HDIM), BF),
            jax.ShapeDtypeStruct((4, 2 * ROWS, HDIM), BF),
            jax.ShapeDtypeStruct((4, ROWS, HDIM), BF),
        ),
        in_specs=[pl.BlockSpec(memory_space=pl.ANY)] * 3,
        out_specs=(vmem(),) * 3,
        scratch_shapes=[pltpu.VMEM((ROWS, 20 * HDIM), BF)] * 3
        + [pltpu.SemaphoreType.DMA((12,))],
        compiler_params=pltpu.CompilerParams(vmem_limit_bytes=60 * 1024 * 1024),
    )(queries, keys, values)


def pack_kernel(kv_ref, q0, q1, q2, q3, out_ref):
    for zl in range(4):
        columns = [ref[zl].astype(F32) for ref in (q0, q1, q2, q3)]
        for zh in range(4):
            out_ref[zh * 4 + zl, 0 : 2 * ROWS, :] = kv_ref[zl]
            span = slice(PART * zh, PART * (zh + 1))
            out_ref[zh * 4 + zl, 2 * ROWS : 3 * ROWS, :] = jnp.concatenate(
                [column[span] for column in columns], axis=0
            ).astype(BF)


def pack(kv, columns):
    return pl.pallas_call(
        pack_kernel,
        out_shape=jax.ShapeDtypeStruct((NZ, 3 * ROWS, HDIM), BF),
        in_specs=[vmem()] * 5,
        out_specs=vmem(),
        compiler_params=params(),
    )(kv, *columns)


def dot_t(a, b):
    return lax.dot_general(a, b, (((1,), (1,)), ((), ())), preferred_element_type=F32)


def row_peak(scores):
    top = scores[:, :HDIM]
    for col in range(HDIM, scores.shape[1], HDIM):
        top = jnp.maximum(top, scores[:, col : col + HDIM])
    return jnp.max(top, axis=-1, keepdims=True)


def widened(value):
    return jnp.concatenate([value, jnp.ones(value.shape, BF)], axis=1)


def absorb(query, pieces, peak, total):
    def rows_of(piece, first):
        parts = [
            ref[lo:hi, first : first + ROWS, :].reshape((hi - lo) * ROWS, HDIM)
            for ref, lo, hi in piece
        ]
        return parts[0] if len(parts) == 1 else jnp.concatenate(parts, axis=0)

    scores = dot_t(query, rows_of(pieces[0], 0))
    for index, piece in enumerate(pieces):
        more = index + 1 < len(pieces)
        later = dot_t(query, rows_of(pieces[index + 1], 0)) if more else None
        highest = row_peak(scores) * SCALE2
        value = widened(rows_of(piece, ROWS))
        newest = highest if peak is None else jnp.maximum(peak, highest)
        weights = jnp.exp2(scores * SCALE2 - newest).astype(BF)
        part = jnp.dot(weights, value, preferred_element_type=F32)
        total = part if peak is None else total * jnp.exp2(peak - newest) + part
        peak, scores = newest, later
    return peak, total


def text_part(query, text_key, text_value, text_len):
    text_scores = dot_t(query, text_key) * SCALE2
    usable = lax.broadcasted_iota(jnp.int32, text_scores.shape, 1) < text_len
    text_scores = jnp.where(usable, text_scores, -1e30)
    text_peak = row_peak(text_scores)
    text_weights = jnp.where(usable, jnp.exp2(text_scores - text_peak), 0.0).astype(BF)
    text_total = jnp.dot(text_weights, widened(text_value), preferred_element_type=F32)
    return text_total[:, :HDIM] / text_total[:, HDIM:]


def pieces_of(refs):
    pieces = []
    for ref in refs:
        for lo in range(0, ref.shape[0], 8):
            part = (ref, lo, min(lo + 8, ref.shape[0]))
            if pieces and sum(hi - lo for _, lo, hi in pieces[-1]) < 8:
                pieces[-1].append(part)
            else:
                pieces.append([part])
    return pieces


def first_kernel(q_ref, k0, k1, k2, total_ref, state_ref):
    query = q_ref[...].reshape(4 * ROWS, HDIM)
    peak, total = absorb(query, pieces_of((k0, k1, k2)), None, None)
    total_ref[...] = total[:, :HDIM]
    lane = lax.broadcasted_iota(jnp.int32, (4 * ROWS, HDIM), 1)
    state_ref[...] = jnp.where(lane < 64, peak, total[:, HDIM:])


def second_kernel(info, q_ref, total_ref, state_ref, k3, k4, tk_ref, tv_ref, out_ref):
    query = q_ref[...].reshape(4 * ROWS, HDIM)
    column = pl.ds(pl.multiple_of(info[0] * HDIM, HDIM), HDIM)
    state = state_ref[...]
    peak = state[:, 0:1]
    weight = jnp.broadcast_to(state[:, HDIM - 1 : HDIM], (4 * ROWS, HDIM))
    total = jnp.concatenate([total_ref[...], weight], axis=1)
    peak, total = absorb(query, pieces_of((k3, k4)), peak, total)
    result = total[:, :HDIM] / total[:, HDIM:]
    result = result + text_part(query, tk_ref[:, column], tv_ref[:, column], info[1])
    out_ref[...] = result.astype(BF).reshape(4, ROWS, HDIM)


def shared_kernel(s_ref, p0, p1, p2, p3):
    rows = NZ * PART
    lane = lax.broadcasted_iota(jnp.int32, (rows, HDIM), 1)
    queries = s_ref[:, 2 * ROWS : 3 * ROWS, :].astype(F32)
    for column, out_ref in enumerate((p0, p1, p2, p3)):
        query = queries[:, PART * column : PART * (column + 1)].reshape(rows, HDIM).astype(BF)
        peak, total = absorb(query, pieces_of((s_ref,)), None, None)
        out_ref[:, 0:HDIM] = (total[:, :HDIM] / total[:, HDIM:]).astype(BF)
        level = peak + jnp.log2(total[:, HDIM:])
        high = level.astype(BF).astype(F32)
        middle = (level - high).astype(BF).astype(F32)
        low = level - high - middle
        terms = jnp.where(lane == 0, high, jnp.where(lane == 1, middle, low))
        out_ref[:, HDIM:] = terms.astype(BF)


def merge_kernel(info, s_ref, p0, p1, p2, p3, tk_ref, tv_ref, out_ref):
    rows = NZ * PART
    query = s_ref[:, 2 * ROWS : 3 * ROWS, :].astype(F32)[:, :PART]
    query = query.reshape(rows, HDIM).astype(BF)
    levels = []
    for ref in (p0, p1, p2, p3):
        terms = ref[:, HDIM:].astype(F32)
        levels.append(terms[:, 0:1] + terms[:, 1:2] + terms[:, 2:3])
    top = functools.reduce(jnp.maximum, levels)
    weights = [jnp.exp2(level - top) for level in levels]
    result = sum(
        weight * ref[:, 0:HDIM].astype(F32) for weight, ref in zip(weights, (p0, p1, p2, p3))
    ) / sum(weights)
    column = slice(4 * HDIM, 5 * HDIM)
    result = result + text_part(query, tk_ref[:, column], tv_ref[:, column], info[1])
    filler = jnp.zeros((NZ, SLOT - PART, HDIM), F32)
    out_ref[...] = jnp.concatenate([result.reshape(NZ, PART, HDIM), filler], axis=1).astype(BF)


KEYS = 6144


def cost(rows, keys):
    return pl.CostEstimate(
        flops=rows * keys * HDIM * 8,
        bytes_accessed=2 * keys * HDIM * 2,
        transcendentals=rows * keys,
    )


def whole(array):
    return pl.BlockSpec(array.shape, lambda i: (0,) * array.ndim)


def main_first(queries, kv):
    rows = 4 * ROWS
    return pl.pallas_call(
        first_kernel,
        grid=(NZ // 4,),
        out_shape=(
            jax.ShapeDtypeStruct((NZ * ROWS, HDIM), F32),
            jax.ShapeDtypeStruct((NZ * ROWS, HDIM), F32),
        ),
        in_specs=[pl.BlockSpec((4, ROWS, HDIM), lambda i: (i, 2, 0))] + [whole(a) for a in kv],
        out_specs=(
            pl.BlockSpec((rows, HDIM), lambda i: (i, 0)),
            pl.BlockSpec((rows, HDIM), lambda i: (i, 0)),
        ),
        compiler_params=params(),
        cost_estimate=cost(NZ * ROWS, 4608),
    )(queries, *kv)


def main_second(info, queries, total, state, kv, text_keys, text_values):
    rows = 4 * ROWS
    return pl.pallas_call(
        second_kernel,
        grid=(NZ // 4,),
        out_shape=jax.ShapeDtypeStruct((NZ, ROWS, HDIM), BF),
        in_specs=[
            smem(),
            pl.BlockSpec((4, ROWS, HDIM), lambda i: (i, 2, 0)),
            pl.BlockSpec((rows, HDIM), lambda i: (i, 0)),
            pl.BlockSpec((rows, HDIM), lambda i: (i, 0)),
        ]
        + [whole(a) for a in kv]
        + [whole(text_keys), whole(text_values)],
        out_specs=pl.BlockSpec((4, ROWS, HDIM), lambda i: (i, 0, 0)),
        compiler_params=params(),
        cost_estimate=cost(NZ * ROWS, 2048),
    )(info, queries, total, state, *kv, text_keys, text_values)


def shared_attention(shared):
    part = jax.ShapeDtypeStruct((NZ * PART, 2 * HDIM), BF)
    return pl.pallas_call(
        shared_kernel,
        out_shape=(part,) * 4,
        in_specs=[vmem()],
        out_specs=(vmem(),) * 4,
        compiler_params=params(),
        cost_estimate=cost(NZ * ROWS, NZ * ROWS),
    )(shared)


def shared_merge(info, shared, parts, text_keys, text_values):
    return pl.pallas_call(
        merge_kernel,
        out_shape=jax.ShapeDtypeStruct((NZ, SLOT, HDIM), BF),
        in_specs=[smem()] + [vmem()] * 7,
        out_specs=vmem(),
        compiler_params=params(),
        cost_estimate=cost(NZ * PART, TXT),
    )(info, shared, *parts, text_keys, text_values)


def head_kernel(
    back_ref, shared_ref, gain_ref, shift_ref, weight_ref, bias_ref, out_ref
):
    blocks = []
    for head in range(20):
        zl, zh = head // 5, head % 5
        if zh < 4:
            block = back_ref[zh * 4 + zl].astype(F32)
        else:
            parts = [shared_ref[part * 4 + zl].astype(F32)[:PART] for part in range(4)]
            block = jnp.concatenate(parts, axis=0)
        blocks.append(block)
    count = 20 * HDIM
    average = jnp.sum(sum(blocks), axis=-1, keepdims=True) / count
    blocks = [block - average for block in blocks]
    variance = jnp.sum(sum(block * block for block in blocks), axis=-1, keepdims=True) / count
    scale = lax.rsqrt(variance + 1e-06)
    patches = jnp.zeros((ROWS, 64), F32)
    for head in range(20):
        span = slice(head * HDIM, (head + 1) * HDIM)
        normed = (blocks[head] * scale * gain_ref[:, span] + shift_ref[:, span]).astype(BF)
        patches = patches + jnp.dot(normed, weight_ref[span, :], preferred_element_type=F32)
    patches = patches + bias_ref[...]
    packed = jnp.concatenate([patches[: ROWS // 2], patches[ROWS // 2 :]], axis=1).astype(BF)
    for copy in range(NZ):
        out_ref[copy] = packed


def head(back, shared, mod_gain, mod_shift, head_weight, head_bias):
    return pl.pallas_call(
        head_kernel,
        out_shape=jax.ShapeDtypeStruct((NZ, ROWS // 2, HDIM), BF),
        in_specs=[vmem()] * 6,
        out_specs=vmem(),
        compiler_params=params(),
    )(back, shared, mod_gain[None], mod_shift[None], head_weight, head_bias[None])


SLAB = 72


def slab_kernel(info, line_ref, out_ref):
    zl = info[3]
    for zh in range(4):
        own = line_ref[zh * 4 + zl].astype(F32)
        above = line_ref[zh * 4 + jnp.maximum(zl - 1, 0)].astype(F32)[PCOL:, 64:]
        below = line_ref[zh * 4 + jnp.minimum(zl + 1, 3)].astype(F32)[:PCOL, :64]
        above = jnp.where(zl > 0, above, 0.0)
        below = jnp.where(zl < 3, below, 0.0)
        left = jnp.concatenate([above, own[:, :64]], axis=0)
        right = jnp.concatenate([own[:, 64:], below], axis=0)
        packed = jnp.concatenate([left, right], axis=1).astype(BF)
        for copy in range(4):
            out_ref[copy, zh] = packed


def slab_of(info, line):
    return pl.pallas_call(
        slab_kernel,
        out_shape=jax.ShapeDtypeStruct((4, 4, SLAB, HDIM), BF),
        in_specs=[smem(), vmem()],
        out_specs=vmem(),
        compiler_params=params(),
    )(info, line)


def conv_kernel(
    info, tile_map, slab_ref, weight_ref, bias_ref, gain_ref, out_ref, wide_ref, pix_ref
):
    wide_ref[...] = jnp.zeros_like(wide_ref)
    for a in range(3):
        for di in (-1, 0, 1):
            for dj in (-1, 0, 1):
                for p in range(2):
                    for q in range(2):
                        row = ((dj + 1) * 4 + p * 2 + q) * LAT
                        for pp in range(2):
                            for qq in range(2):
                                r = 2 * di + p - pp + 1
                                s = 2 * dj + q - qq + 1
                                if 0 <= r < 3 and 0 <= s < 3:
                                    tap = ((a * 3 + r) * 3 + s) * LAT
                                    col = (pp * 2 + qq) * C_OUT
                                    wide_ref[
                                        a * 3 + di + 1, row : row + LAT, col : col + C_OUT
                                    ] = weight_ref[tap : tap + LAT, :]
    x, zh = info[2], info[0]
    pre = jnp.zeros((ROWS, 4 * C_OUT), F32)
    column = lax.broadcasted_iota(jnp.int32, (6 * PCOL, 64), 0) % PCOL
    for a in range(3):
        wanted = 4 * x + zh - 2 + a
        source = jnp.int32(0)
        for b in range(16):
            source = jnp.where(tile_map[b] == wanted, b, source)
        slab = slab_ref[source].astype(F32)
        slab = jnp.concatenate([slab[:, :64], slab[:, 64:]], axis=0)
        slab = jnp.where(wanted >= 0, slab, 0.0)
        zero = jnp.zeros((8, 64), F32)
        tall = jnp.concatenate([zero, slab, zero], axis=0)
        left = jnp.where(column == 0, 0.0, tall[7 : 7 + 6 * PCOL])
        right = jnp.where(column == PCOL - 1, 0.0, tall[9 : 9 + 6 * PCOL])
        joined = jnp.concatenate([left, slab, right], axis=1)
        for di in range(3):
            part = joined[di * PCOL : di * PCOL + ROWS].astype(BF)
            pre = pre + jnp.dot(part, wide_ref[a * 3 + di], preferred_element_type=F32)
    for pp in range(2):
        for qq in range(2):
            at = (pp * 2 + qq) * C_OUT
            value = pre[:, at : at + C_OUT] + bias_ref[...]
            mean = jnp.mean(value * value, axis=-1, keepdims=True)
            value = value * lax.rsqrt(mean + 1e-06) * gain_ref[...]
            value = value / (1.0 + jnp.exp(-value))
            for i in range(4):
                for part in range(3):
                    pix_ref[part, 2 * i + pp, pl.ds(qq, PCOL, 2), :] = value[
                        i * PCOL : (i + 1) * PCOL, part * HDIM : (part + 1) * HDIM
                    ]
    for part in range(3):
        out_ref[:, :, part * HDIM : (part + 1) * HDIM] = pix_ref[part].astype(BF)


def conv(info, tile_map, gathered, conv_weight, conv_bias, norm_gain):
    return pl.pallas_call(
        conv_kernel,
        out_shape=jax.ShapeDtypeStruct((8, 48, C_OUT), BF),
        in_specs=[smem(), smem()] + [vmem()] * 4,
        out_specs=vmem(),
        scratch_shapes=[
            pltpu.VMEM((9, 192, 4 * C_OUT), BF),
            pltpu.VMEM((3, 8, 48, HDIM), F32),
        ],
        compiler_params=params(),
    )(info, tile_map, gathered, conv_weight, conv_bias[None], norm_gain[None])


def shift(block, axis, distance):
    return lax.ppermute(block, axis, [(i, (i + distance) % 4) for i in range(4)])


def around(block, axis):
    right = shift(block, axis, 1)
    left = shift(block, axis, -1)
    half = block.shape[0] // 2
    return (block, right, left, shift(right[:half], axis, 1), shift(left[half:], axis, -1))


def exchange(block, axis):
    return lax.all_to_all(block, axis, split_axis=0, concat_axis=0, tiled=True)


def per_device(
    queries,
    keys,
    values,
    text_keys,
    text_values,
    text_len,
    tile_map,
    mod_gain,
    mod_shift,
    head_weight,
    head_bias,
    conv_weight,
    conv_bias,
    norm_gain,
):
    x, zh, zl = (lax.axis_index(axis) for axis in ("x", "zh", "zl"))
    info = jnp.stack([zh, text_len[0], x, zl]).astype(jnp.int32)
    main_send, last_kv, last_q = load(queries, keys, values)
    columns = [last_q] + [shift(last_q, "x", distance) for distance in (1, 2, 3)]
    main = exchange(main_send, Z)
    main, shared_send = lax.optimization_barrier((main, pack(last_kv, columns)))
    shared = exchange(shared_send, Z)
    main_kv = (main,) + around(main[:, : 2 * ROWS], "x")[1:]
    total, state = main_first(main, main_kv[:3])
    out = main_second(info, main, total, state, main_kv[3:], text_keys, text_values)
    out, shared = lax.optimization_barrier((out, shared))
    back = exchange(out, Z)
    parts = shared_attention(shared)
    parts = [parts[0]] + [shift(parts[distance], "x", -distance) for distance in (1, 2, 3)]
    merged = shared_merge(info, shared, parts, text_keys, text_values)
    back, merged = lax.optimization_barrier((back, merged))
    shared_back = exchange(merged, Z)
    line = exchange(head(back, shared_back, mod_gain, mod_shift, head_weight, head_bias), Z)
    plane = exchange(slab_of(info, line), "x")
    gathered = plane.reshape(16, SLAB, HDIM)
    out = conv(info, tile_map, gathered, conv_weight, conv_bias, norm_gain)
    return out[None]


def solution(mesh):
    inner = Mesh(mesh.devices.reshape(8, 4, 4, 4), ("clip", "x", "zh", "zl"))
    tokens = P(("clip", "x", "zh", "zl"), None)
    placed = (
        tokens,
        tokens,
        tokens,
        P("clip", "zl"),
        P("clip", "zl"),
        P("clip"),
        P("clip"),
    ) + (P(),) * 7
    return jax.shard_map(
        per_device,
        mesh=inner,
        in_specs=placed,
        out_specs=P(("clip", "x", "zh"), "zl", None, None),
        check_vma=False,
    )
```

```python
import functools

import jax
import jax.numpy as jnp
from jax import lax
from jax.experimental import pallas as pl
from jax.experimental.pallas import tpu as pltpu
from jax.sharding import Mesh, PartitionSpec as P

PCOL = 24
HDIM = 128
TXT = 512
LAT = 16
ROWS = 96
NZ = 16
C_OUT = 384
LOG2E = 1.4426950408889634
SCALE2 = HDIM ** (-0.5) * LOG2E
Z = ("zh", "zl")
F32 = jnp.float32
BF = jnp.bfloat16
VMEM_LIMIT = 50 * 1024 * 1024


def params():
    return pltpu.CompilerParams(vmem_limit_bytes=VMEM_LIMIT)


def vmem():
    return pl.BlockSpec(memory_space=pltpu.VMEM)


def smem():
    return pl.BlockSpec(memory_space=pltpu.SMEM)


def load_kernel(
    q_hbm, k_hbm, v_hbm, main_out, kv_out, last_out, q_ref, k_ref, v_ref, sems
):
    width = 5 * HDIM
    copies = []
    for zl in range(4):
        span = slice(zl * width, (zl + 1) * width)
        for index, (source, target) in enumerate(((k_hbm, k_ref), (v_hbm, v_ref), (q_hbm, q_ref))):
            copy = pltpu.make_async_copy(
                source.at[:, span], target.at[:, span], sems.at[3 * zl + index]
            )
            copy.start()
            copies.append(copy)
    for zl in range(4):
        for copy in copies[3 * zl : 3 * zl + 3]:
            copy.wait()
        last = slice((5 * zl + 4) * HDIM, (5 * zl + 5) * HDIM)
        for index, ref in enumerate((k_ref, v_ref, q_ref)):
            rows = slice(index * ROWS, (index + 1) * ROWS)
            for zh in range(4):
                own = slice((5 * zl + zh) * HDIM, (5 * zl + zh + 1) * HDIM)
                main_out[zh * 4 + zl, rows, :] = ref[:, own]
                if index < 2:
                    kv_out[zh * 4 + zl, rows, :] = ref[:, last]
    for distance in range(4):
        group = lax.rem(lax.axis_index("zl") + distance, 4)
        span = pl.ds(pl.multiple_of((5 * group + 4) * HDIM, HDIM), HDIM)
        last_out[distance] = q_ref[:, span]


def load(queries, keys, values):
    return pl.pallas_call(
        load_kernel,
        out_shape=(
            jax.ShapeDtypeStruct((NZ, 3 * ROWS, HDIM), BF),
            jax.ShapeDtypeStruct((NZ, 2 * ROWS, HDIM), BF),
            jax.ShapeDtypeStruct((4, ROWS, HDIM), BF),
        ),
        in_specs=[pl.BlockSpec(memory_space=pl.ANY)] * 3,
        out_specs=(vmem(),) * 3,
        scratch_shapes=[pltpu.VMEM((ROWS, 20 * HDIM), BF)] * 3
        + [pltpu.SemaphoreType.DMA((12,))],
        compiler_params=pltpu.CompilerParams(vmem_limit_bytes=60 * 1024 * 1024),
    )(queries, keys, values)


def dot_t(a, b):
    return lax.dot_general(a, b, (((1,), (1,)), ((), ())), preferred_element_type=F32)


def row_peak(scores):
    top = scores[:, :HDIM]
    for col in range(HDIM, scores.shape[1], HDIM):
        top = jnp.maximum(top, scores[:, col : col + HDIM])
    return jnp.max(top, axis=-1, keepdims=True)


def widened(value):
    return jnp.concatenate([value, jnp.ones(value.shape, BF)], axis=1)


def absorb(query, pieces, peak, total):
    def rows_of(piece, first):
        parts = [
            ref[lo:hi, first : first + ROWS, :].reshape((hi - lo) * ROWS, HDIM)
            for ref, lo, hi in piece
        ]
        return parts[0] if len(parts) == 1 else jnp.concatenate(parts, axis=0)

    scores = dot_t(query, rows_of(pieces[0], 0))
    for index, piece in enumerate(pieces):
        more = index + 1 < len(pieces)
        later = dot_t(query, rows_of(pieces[index + 1], 0)) if more else None
        highest = row_peak(scores) * SCALE2
        value = widened(rows_of(piece, ROWS))
        newest = highest if peak is None else jnp.maximum(peak, highest)
        weights = jnp.exp2(scores * SCALE2 - newest).astype(BF)
        part = jnp.dot(weights, value, preferred_element_type=F32)
        total = part if peak is None else total * jnp.exp2(peak - newest) + part
        peak, scores = newest, later
    return peak, total


def text_part(query, text_key, text_value, text_len):
    text_scores = dot_t(query, text_key) * SCALE2
    usable = lax.broadcasted_iota(jnp.int32, text_scores.shape, 1) < text_len
    text_scores = jnp.where(usable, text_scores, -1e30)
    text_peak = row_peak(text_scores)
    text_weights = jnp.where(usable, jnp.exp2(text_scores - text_peak), 0.0).astype(BF)
    text_total = jnp.dot(text_weights, widened(text_value), preferred_element_type=F32)
    return text_total[:, :HDIM] / text_total[:, HDIM:]


def pieces_of(refs):
    pieces = []
    for ref in refs:
        for lo in range(0, ref.shape[0], 8):
            part = (ref, lo, min(lo + 8, ref.shape[0]))
            if pieces and sum(hi - lo for _, lo, hi in pieces[-1]) < 8:
                pieces[-1].append(part)
            else:
                pieces.append([part])
    return pieces


def put_state(peak, total, total_ref, state_ref):
    total_ref[...] = total[:, :HDIM]
    lane = lax.broadcasted_iota(jnp.int32, total_ref.shape, 1)
    state_ref[...] = jnp.where(lane < 64, peak, total[:, HDIM:])


def get_state(total_ref, state_ref):
    state = state_ref[...]
    weight = jnp.broadcast_to(state[:, HDIM - 1 : HDIM], state.shape)
    return state[:, 0:1], jnp.concatenate([total_ref[...], weight], axis=1)


def own_kernel(info, q_ref, k0, tk_ref, tv_ref, total_ref, state_ref, text_ref):
    query = q_ref[...].reshape(GROUP * ROWS, HDIM)
    column = pl.ds(pl.multiple_of(info[0] * HDIM, HDIM), HDIM)
    text_ref[...] = text_part(query, tk_ref[:, column], tv_ref[:, column], info[1])
    put_state(*absorb(query, pieces_of((k0,)), None, None), total_ref, state_ref)


def near_kernel(q_ref, total_in, state_in, k1, k2, total_ref, state_ref):
    query = q_ref[...].reshape(GROUP * ROWS, HDIM)
    state = get_state(total_in, state_in)
    put_state(*absorb(query, pieces_of((k1, k2)), *state), total_ref, state_ref)


def far_kernel(q_ref, total_in, state_in, text_in, k3, k4, out_ref):
    query = q_ref[...].reshape(GROUP * ROWS, HDIM)
    state = get_state(total_in, state_in)
    peak, total = absorb(query, pieces_of((k3, k4)), *state)
    result = total[:, :HDIM] / total[:, HDIM:] + text_in[...]
    out_ref[...] = result.astype(BF).reshape(GROUP, ROWS, HDIM)


def shared_kernel(kv_ref, q0, q1, q2, q3, p0, p1, p2, p3):
    rows = 4 * ROWS
    lane = lax.broadcasted_iota(jnp.int32, (rows, HDIM), 1)
    for column, out_ref in enumerate((p0, p1, p2, p3)):
        query = jnp.concatenate([ref[column] for ref in (q0, q1, q2, q3)], axis=0)
        peak, total = absorb(query, pieces_of((kv_ref,)), None, None)
        out_ref[:, 0:HDIM] = (total[:, :HDIM] / total[:, HDIM:]).astype(BF)
        level = peak + jnp.log2(total[:, HDIM:])
        high = level.astype(BF).astype(F32)
        middle = (level - high).astype(BF).astype(F32)
        low = level - high - middle
        terms = jnp.where(lane == 0, high, jnp.where(lane == 1, middle, low))
        out_ref[:, HDIM:] = terms.astype(BF)


def merge_kernel(info, q0, q1, q2, q3, p0, p1, p2, p3, tk_ref, tv_ref, out_ref):
    query = jnp.concatenate([ref[0] for ref in (q0, q1, q2, q3)], axis=0)
    levels = []
    for ref in (p0, p1, p2, p3):
        terms = ref[:, HDIM:].astype(F32)
        levels.append(terms[:, 0:1] + terms[:, 1:2] + terms[:, 2:3])
    top = functools.reduce(jnp.maximum, levels)
    weights = [jnp.exp2(level - top) for level in levels]
    result = sum(
        weight * ref[:, 0:HDIM].astype(F32) for weight, ref in zip(weights, (p0, p1, p2, p3))
    ) / sum(weights)
    column = slice(4 * HDIM, 5 * HDIM)
    result = result + text_part(query, tk_ref[:, column], tv_ref[:, column], info[1])
    for distance in range(4):
        rows = slice(distance * ROWS, (distance + 1) * ROWS)
        out_ref[lax.rem(info[3] + 4 - distance, 4)] = result[rows].astype(BF)


KEYS = 6144


def cost(rows, keys):
    return pl.CostEstimate(
        flops=rows * keys * HDIM * 8,
        bytes_accessed=2 * keys * HDIM * 2,
        transcendentals=rows * keys,
    )


GROUP = 4
QUERY_BLOCK = pl.BlockSpec((GROUP, ROWS, HDIM), lambda i: (i, 2, 0))
STATE_BLOCK = pl.BlockSpec((GROUP * ROWS, HDIM), lambda i: (i, 0))
STATE = jax.ShapeDtypeStruct((NZ * ROWS, HDIM), F32)


def main_own(info, main, text_keys, text_values):
    return pl.pallas_call(
        own_kernel,
        grid=(NZ // GROUP,),
        out_shape=(STATE,) * 3,
        in_specs=[smem(), QUERY_BLOCK, vmem(), vmem(), vmem()],
        out_specs=(STATE_BLOCK,) * 3,
        compiler_params=params(),
        cost_estimate=cost(NZ * ROWS, NZ * ROWS + TXT),
    )(info, main, main, text_keys, text_values)


def main_near(main, total, state, kv):
    return pl.pallas_call(
        near_kernel,
        grid=(NZ // GROUP,),
        out_shape=(STATE,) * 2,
        in_specs=[QUERY_BLOCK, STATE_BLOCK, STATE_BLOCK] + [vmem()] * len(kv),
        out_specs=(STATE_BLOCK,) * 2,
        compiler_params=params(),
        cost_estimate=cost(NZ * ROWS, 2 * NZ * ROWS),
    )(main, total, state, *kv)


def main_far(main, total, state, text, kv):
    return pl.pallas_call(
        far_kernel,
        grid=(NZ // GROUP,),
        out_shape=jax.ShapeDtypeStruct((NZ, ROWS, HDIM), BF),
        in_specs=[QUERY_BLOCK] + [STATE_BLOCK] * 3 + [vmem()] * len(kv),
        out_specs=pl.BlockSpec((GROUP, ROWS, HDIM), lambda i: (i, 0, 0)),
        compiler_params=params(),
        cost_estimate=cost(NZ * ROWS, NZ * ROWS),
    )(main, total, state, text, *kv)


def shared_attention(kv, columns):
    part = jax.ShapeDtypeStruct((4 * ROWS, 2 * HDIM), BF)
    return pl.pallas_call(
        shared_kernel,
        out_shape=(part,) * 4,
        in_specs=[vmem()] * 5,
        out_specs=(vmem(),) * 4,
        compiler_params=params(),
        cost_estimate=cost(NZ * ROWS, NZ * ROWS),
    )(kv, *columns)


def shared_merge(info, queries, parts, text_keys, text_values):
    return pl.pallas_call(
        merge_kernel,
        out_shape=jax.ShapeDtypeStruct((4, ROWS, HDIM), BF),
        in_specs=[smem()] + [vmem()] * 10,
        out_specs=vmem(),
        compiler_params=params(),
        cost_estimate=cost(4 * ROWS, TXT),
    )(info, *queries, *parts, text_keys, text_values)


def head_kernel(
    back_ref, shared_ref, gain_ref, shift_ref, weight_ref, bias_ref, out_ref
):
    blocks = []
    for zl in range(4):
        for zh in range(5):
            start = (5 * zl + zh) * HDIM
            block = back_ref[zh * 4 + zl] if zh < 4 else shared_ref[zl]
            blocks.append((block.astype(F32), slice(start, start + HDIM)))
    count = 20 * HDIM
    average = jnp.sum(sum(block for block, _ in blocks), axis=-1, keepdims=True) / count
    blocks = [(block - average, span) for block, span in blocks]
    variance = sum(block * block for block, _ in blocks)
    variance = jnp.sum(variance, axis=-1, keepdims=True) / count
    scale = lax.rsqrt(variance + 1e-06)
    patches = jnp.zeros((ROWS, 64), F32)
    for block, span in blocks:
        normed = (block * scale * gain_ref[:, span] + shift_ref[:, span]).astype(BF)
        patches = patches + jnp.dot(normed, weight_ref[span, :], preferred_element_type=F32)
    patches = patches + bias_ref[...]
    packed = jnp.concatenate([patches[: ROWS // 2], patches[ROWS // 2 :]], axis=1).astype(BF)
    for copy in range(NZ):
        out_ref[copy] = packed


def head(back, shared, mod_gain, mod_shift, head_weight, head_bias):
    return pl.pallas_call(
        head_kernel,
        out_shape=jax.ShapeDtypeStruct((NZ, ROWS // 2, HDIM), BF),
        in_specs=[vmem()] * 6,
        out_specs=vmem(),
        compiler_params=params(),
    )(back, shared, mod_gain[None], mod_shift[None], head_weight, head_bias[None])


SLAB = 72


def slab_kernel(info, line_ref, out_ref):
    zl = info[3]
    for zh in range(4):
        own = line_ref[zh * 4 + zl].astype(F32)
        above = line_ref[zh * 4 + jnp.maximum(zl - 1, 0)].astype(F32)[PCOL:, 64:]
        below = line_ref[zh * 4 + jnp.minimum(zl + 1, 3)].astype(F32)[:PCOL, :64]
        above = jnp.where(zl > 0, above, 0.0)
        below = jnp.where(zl < 3, below, 0.0)
        left = jnp.concatenate([above, own[:, :64]], axis=0)
        right = jnp.concatenate([own[:, 64:], below], axis=0)
        packed = jnp.concatenate([left, right], axis=1).astype(BF)
        for copy in range(4):
            out_ref[copy, zh] = packed


def slab_of(info, line):
    return pl.pallas_call(
        slab_kernel,
        out_shape=jax.ShapeDtypeStruct((4, 4, SLAB, HDIM), BF),
        in_specs=[smem(), vmem()],
        out_specs=vmem(),
        compiler_params=params(),
    )(info, line)


def conv_kernel(
    info, tile_map, slab_ref, weight_ref, bias_ref, gain_ref, out_ref, wide_ref, pix_ref
):
    wide_ref[...] = jnp.zeros_like(wide_ref)
    for a in range(3):
        for di in (-1, 0, 1):
            for dj in (-1, 0, 1):
                for p in range(2):
                    for q in range(2):
                        row = ((dj + 1) * 4 + p * 2 + q) * LAT
                        for pp in range(2):
                            for qq in range(2):
                                r = 2 * di + p - pp + 1
                                s = 2 * dj + q - qq + 1
                                if 0 <= r < 3 and 0 <= s < 3:
                                    tap = ((a * 3 + r) * 3 + s) * LAT
                                    col = (pp * 2 + qq) * C_OUT
                                    wide_ref[
                                        a * 3 + di + 1, row : row + LAT, col : col + C_OUT
                                    ] = weight_ref[tap : tap + LAT, :]
    x, zh = info[2], info[0]
    pre = jnp.zeros((ROWS, 4 * C_OUT), F32)
    column = lax.broadcasted_iota(jnp.int32, (6 * PCOL, 64), 0) % PCOL
    for a in range(3):
        wanted = 4 * x + zh - 2 + a
        source = jnp.int32(0)
        for b in range(16):
            source = jnp.where(tile_map[b] == wanted, b, source)
        slab = slab_ref[source].astype(F32)
        slab = jnp.concatenate([slab[:, :64], slab[:, 64:]], axis=0)
        slab = jnp.where(wanted >= 0, slab, 0.0)
        zero = jnp.zeros((8, 64), F32)
        tall = jnp.concatenate([zero, slab, zero], axis=0)
        left = jnp.where(column == 0, 0.0, tall[7 : 7 + 6 * PCOL])
        right = jnp.where(column == PCOL - 1, 0.0, tall[9 : 9 + 6 * PCOL])
        joined = jnp.concatenate([left, slab, right], axis=1)
        for di in range(3):
            part = joined[di * PCOL : di * PCOL + ROWS].astype(BF)
            pre = pre + jnp.dot(part, wide_ref[a * 3 + di], preferred_element_type=F32)
    for pp in range(2):
        for qq in range(2):
            at = (pp * 2 + qq) * C_OUT
            value = pre[:, at : at + C_OUT] + bias_ref[...]
            mean = jnp.mean(value * value, axis=-1, keepdims=True)
            value = value * lax.rsqrt(mean + 1e-06) * gain_ref[...]
            value = value / (1.0 + jnp.exp(-value))
            for i in range(4):
                for part in range(3):
                    pix_ref[part, 2 * i + pp, pl.ds(qq, PCOL, 2), :] = value[
                        i * PCOL : (i + 1) * PCOL, part * HDIM : (part + 1) * HDIM
                    ]
    for part in range(3):
        out_ref[:, :, part * HDIM : (part + 1) * HDIM] = pix_ref[part].astype(BF)


def conv(info, tile_map, gathered, conv_weight, conv_bias, norm_gain):
    return pl.pallas_call(
        conv_kernel,
        out_shape=jax.ShapeDtypeStruct((8, 48, C_OUT), BF),
        in_specs=[smem(), smem()] + [vmem()] * 4,
        out_specs=vmem(),
        scratch_shapes=[
            pltpu.VMEM((9, 192, 4 * C_OUT), BF),
            pltpu.VMEM((3, 8, 48, HDIM), F32),
        ],
        compiler_params=params(),
    )(info, tile_map, gathered, conv_weight, conv_bias[None], norm_gain[None])


def shift(block, axis, distance):
    return lax.ppermute(block, axis, [(i, (i + distance) % 4) for i in range(4)])


def around(block, axis):
    right = shift(block, axis, 1)
    left = shift(block, axis, -1)
    half = block.shape[0] // 2
    return (right, left), (shift(right[:half], axis, 1), shift(left[half:], axis, -1))


def exchange(block, axis):
    return lax.all_to_all(block, axis, split_axis=0, concat_axis=0, tiled=True)


def per_device(
    queries,
    keys,
    values,
    text_keys,
    text_values,
    text_len,
    tile_map,
    mod_gain,
    mod_shift,
    head_weight,
    head_bias,
    conv_weight,
    conv_bias,
    norm_gain,
):
    x, zh, zl = (lax.axis_index(axis) for axis in ("x", "zh", "zl"))
    info = jnp.stack([zh, text_len[0], x, zl]).astype(jnp.int32)
    main_send, shared_send, last = load(queries, keys, values)
    last = jnp.stack([last] + [shift(last, "x", d) for d in (1, 2, 3)], axis=1)
    last = [last[0]] + [shift(last[d], "zl", d) for d in (1, 2, 3)]
    main = exchange(main_send, Z)
    main, last, shared_send = lax.optimization_barrier((main, last, shared_send))
    shared = exchange(shared_send, Z)
    near, far = around(main[:, : 2 * ROWS], "x")
    total, state, text = main_own(info, main, text_keys, text_values)
    total, state = main_near(main, total, state, near)
    out = main_far(main, total, state, text, far)
    out, shared = lax.optimization_barrier((out, shared))
    back = exchange(out, Z)
    parts = shared_attention(shared, last)
    parts = [parts[0]] + [shift(parts[d], "x", -d) for d in (1, 2, 3)]
    merged = shared_merge(info, last, parts, text_keys, text_values)
    back, merged = lax.optimization_barrier((back, merged))
    shared_back = exchange(merged, "zl")
    line = head(back, shared_back, mod_gain, mod_shift, head_weight, head_bias)
    line = exchange(line, Z)
    plane = exchange(slab_of(info, line), "x")
    gathered = plane.reshape(16, SLAB, HDIM)
    out = conv(info, tile_map, gathered, conv_weight, conv_bias, norm_gain)
    return out[None]


def solution(mesh):
    inner = Mesh(mesh.devices.reshape(8, 4, 4, 4), ("clip", "x", "zh", "zl"))
    tokens = P(("clip", "x", "zh", "zl"), None)
    placed = (
        tokens,
        tokens,
        tokens,
        P("clip", "zl"),
        P("clip", "zl"),
        P("clip"),
        P("clip"),
    ) + (P(),) * 7
    return jax.shard_map(
        per_device,
        mesh=inner,
        in_specs=placed,
        out_specs=P(("clip", "x", "zh"), "zl", None, None),
        check_vma=False,
    )
```

```python
import functools

import jax
import jax.numpy as jnp
from jax import lax
from jax.experimental import pallas as pl
from jax.experimental.pallas import tpu as pltpu
from jax.sharding import Mesh, PartitionSpec as P

PCOL = 24
HDIM = 128
TXT = 512
LAT = 16
ROWS = 96
NZ = 16
C_OUT = 384
LOG2E = 1.4426950408889634
SCALE2 = HDIM ** (-0.5) * LOG2E
Z = ("zh", "zl")
F32 = jnp.float32
BF = jnp.bfloat16
VMEM_LIMIT = 50 * 1024 * 1024


def params():
    return pltpu.CompilerParams(vmem_limit_bytes=VMEM_LIMIT)


def vmem():
    return pl.BlockSpec(memory_space=pltpu.VMEM)


def smem():
    return pl.BlockSpec(memory_space=pltpu.SMEM)


def load_kernel(
    q_hbm, k_hbm, v_hbm, main_out, kv_out, last_out, q_ref, k_ref, v_ref, sems
):
    width = 5 * HDIM
    copies = []
    for zl in range(4):
        span = slice(zl * width, (zl + 1) * width)
        for index, (source, target) in enumerate(((k_hbm, k_ref), (v_hbm, v_ref), (q_hbm, q_ref))):
            copy = pltpu.make_async_copy(
                source.at[:, span], target.at[:, span], sems.at[3 * zl + index]
            )
            copy.start()
            copies.append(copy)
    for zl in range(4):
        for copy in copies[3 * zl : 3 * zl + 3]:
            copy.wait()
        last = slice((5 * zl + 4) * HDIM, (5 * zl + 5) * HDIM)
        for index, ref in enumerate((k_ref, v_ref, q_ref)):
            rows = slice(index * ROWS, (index + 1) * ROWS)
            for zh in range(4):
                own = slice((5 * zl + zh) * HDIM, (5 * zl + zh + 1) * HDIM)
                main_out[zh * 4 + zl, rows, :] = ref[:, own]
                if index < 2:
                    kv_out[zh * 4 + zl, rows, :] = ref[:, last]
    for distance in range(4):
        group = lax.rem(lax.axis_index("zl") + distance, 4)
        span = pl.ds(pl.multiple_of((5 * group + 4) * HDIM, HDIM), HDIM)
        last_out[distance] = q_ref[:, span]


def load(queries, keys, values):
    return pl.pallas_call(
        load_kernel,
        out_shape=(
            jax.ShapeDtypeStruct((NZ, 3 * ROWS, HDIM), BF),
            jax.ShapeDtypeStruct((NZ, 2 * ROWS, HDIM), BF),
            jax.ShapeDtypeStruct((4, ROWS, HDIM), BF),
        ),
        in_specs=[pl.BlockSpec(memory_space=pl.ANY)] * 3,
        out_specs=(vmem(),) * 3,
        scratch_shapes=[pltpu.VMEM((ROWS, 20 * HDIM), BF)] * 3
        + [pltpu.SemaphoreType.DMA((12,))],
        compiler_params=pltpu.CompilerParams(vmem_limit_bytes=60 * 1024 * 1024),
    )(queries, keys, values)


def dot_t(a, b):
    return lax.dot_general(a, b, (((1,), (1,)), ((), ())), preferred_element_type=F32)


def row_peak(scores):
    top = scores[:, :HDIM]
    for col in range(HDIM, scores.shape[1], HDIM):
        top = jnp.maximum(top, scores[:, col : col + HDIM])
    return jnp.max(top, axis=-1, keepdims=True)


def widened(value):
    return jnp.concatenate([value, jnp.ones(value.shape, BF)], axis=1)


def rows_of(piece, first):
    parts = [
        ref[lo:hi, first : first + ROWS, :].reshape((hi - lo) * ROWS, HDIM)
        for ref, lo, hi in piece
    ]
    return parts[0] if len(parts) == 1 else jnp.concatenate(parts, axis=0)


def absorb(groups, pieces, begin, finish):
    steps = [(group, piece) for group in range(len(groups)) for piece in range(len(pieces))]

    def scores_of(step):
        return dot_t(groups[step[0]](), rows_of(pieces[step[1]], 0))

    scores = scores_of(steps[0])
    for index, (group, piece) in enumerate(steps):
        if piece == 0:
            peak, total = begin(group)
        later = scores_of(steps[index + 1]) if index + 1 < len(steps) else None
        highest = row_peak(scores) * SCALE2
        value = widened(rows_of(pieces[piece], ROWS))
        newest = highest if peak is None else jnp.maximum(peak, highest)
        weights = jnp.exp2(scores * SCALE2 - newest).astype(BF)
        part = jnp.dot(weights, value, preferred_element_type=F32)
        total = part if peak is None else total * jnp.exp2(peak - newest) + part
        peak, scores = newest, later
        if piece + 1 == len(pieces):
            finish(group, peak, total)


def fresh(group):
    return None, None


def text_part(query, text_key, text_value, text_len):
    text_scores = dot_t(query, text_key) * SCALE2
    usable = lax.broadcasted_iota(jnp.int32, text_scores.shape, 1) < text_len
    text_scores = jnp.where(usable, text_scores, -1e30)
    text_peak = row_peak(text_scores)
    text_weights = jnp.where(usable, jnp.exp2(text_scores - text_peak), 0.0).astype(BF)
    text_total = jnp.dot(text_weights, widened(text_value), preferred_element_type=F32)
    return text_total[:, :HDIM] / text_total[:, HDIM:]


def pieces_of(refs):
    pieces = []
    for ref in refs:
        for lo in range(0, ref.shape[0], 8):
            part = (ref, lo, min(lo + 8, ref.shape[0]))
            if pieces and sum(hi - lo for _, lo, hi in pieces[-1]) < 8:
                pieces[-1].append(part)
            else:
                pieces.append([part])
    return pieces


GROUP = 4


def rows_in(group):
    return slice(group * GROUP * ROWS, (group + 1) * GROUP * ROWS)


def sources_in(group):
    return slice(group * GROUP, (group + 1) * GROUP)


def queries_of(main_ref):
    def query(group):
        part = main_ref[sources_in(group), 2 * ROWS : 3 * ROWS, :]
        return part.reshape(GROUP * ROWS, HDIM)

    return [functools.partial(query, group) for group in range(NZ // GROUP)]


def state_to(total_ref, state_ref):
    def finish(group, peak, total):
        total_ref[rows_in(group), :] = total[:, :HDIM]
        lane = lax.broadcasted_iota(jnp.int32, (GROUP * ROWS, HDIM), 1)
        state_ref[rows_in(group), :] = jnp.where(lane < 64, peak, total[:, HDIM:])

    return finish


def state_from(total_ref, state_ref):
    def begin(group):
        state = state_ref[rows_in(group), :]
        weight = jnp.broadcast_to(state[:, HDIM - 1 : HDIM], state.shape)
        return state[:, 0:1], jnp.concatenate([total_ref[rows_in(group), :], weight], axis=1)

    return begin


def own_kernel(info, main_ref, tk_ref, tv_ref, total_ref, state_ref, text_ref):
    column = pl.ds(pl.multiple_of(info[0] * HDIM, HDIM), HDIM)
    queries = queries_of(main_ref)
    absorb(queries, pieces_of((main_ref,)), fresh, state_to(total_ref, state_ref))
    for group, query in enumerate(queries):
        text = text_part(query(), tk_ref[:, column], tv_ref[:, column], info[1])
        text_ref[rows_in(group), :] = text


def near_kernel(main_ref, total_in, state_in, k1, k2, total_ref, state_ref):
    begin, finish = state_from(total_in, state_in), state_to(total_ref, state_ref)
    absorb(queries_of(main_ref), pieces_of((k1, k2)), begin, finish)


def far_kernel(main_ref, total_in, state_in, text_in, k3, k4, out_ref):
    def finish(group, peak, total):
        result = total[:, :HDIM] / total[:, HDIM:] + text_in[rows_in(group), :]
        out_ref[sources_in(group)] = result.astype(BF).reshape(GROUP, ROWS, HDIM)

    begin = state_from(total_in, state_in)
    absorb(queries_of(main_ref), pieces_of((k3, k4)), begin, finish)


PART_ROWS = 4 * ROWS + 3 * 16


def shared_kernel(kv_ref, q0, q1, q2, q3, p0, p1, p2, p3):
    rows = 4 * ROWS
    line = lax.broadcasted_iota(jnp.int32, (16, rows), 0)
    outs = (p0, p1, p2, p3)

    def query(column):
        return jnp.concatenate([ref[column] for ref in (q0, q1, q2, q3)], axis=0)

    def finish(column, peak, total):
        outs[column][0:rows] = (total[:, :HDIM] / total[:, HDIM:]).astype(BF)
        level = jnp.transpose(peak + jnp.log2(total[:, HDIM:]))[0:16]
        high = level.astype(BF).astype(F32)
        middle = (level - high).astype(BF).astype(F32)
        low = level - high - middle
        terms = jnp.where(line == 0, high, jnp.where(line == 1, middle, low)).astype(BF)
        for part in range(3):
            start = rows + 16 * part
            outs[column][start : start + 16] = terms[:, part * HDIM : (part + 1) * HDIM]

    queries = [functools.partial(query, column) for column in range(4)]
    absorb(queries, pieces_of((kv_ref,)), fresh, finish)


def level_of(ref):
    columns = []
    for part in range(3):
        start = 4 * ROWS + 16 * part
        terms = ref[start : start + 16].astype(F32)
        level = terms[0:1] + terms[1:2] + terms[2:3]
        columns.append(jnp.transpose(jnp.broadcast_to(level, (HDIM, HDIM))))
    return jnp.concatenate(columns, axis=0)


def merge_kernel(info, q0, q1, q2, q3, p0, p1, p2, p3, tk_ref, tv_ref, out_ref):
    query = jnp.concatenate([ref[0] for ref in (q0, q1, q2, q3)], axis=0)
    parts = (p0, p1, p2, p3)
    levels = [level_of(ref) for ref in parts]
    top = functools.reduce(jnp.maximum, levels)
    weights = [jnp.exp2(level - top) for level in levels]
    result = sum(
        weight * ref[0 : 4 * ROWS].astype(F32) for weight, ref in zip(weights, parts)
    ) / sum(weights)
    column = slice(4 * HDIM, 5 * HDIM)
    result = result + text_part(query, tk_ref[:, column], tv_ref[:, column], info[1])
    for distance in range(4):
        rows = slice(distance * ROWS, (distance + 1) * ROWS)
        out_ref[lax.rem(info[3] + 4 - distance, 4)] = result[rows].astype(BF)


def rows_kernel(main_ref, out_ref):
    out_ref[...] = main_ref[:, 0 : 2 * ROWS, :]


def key_rows(main):
    return pl.pallas_call(
        rows_kernel,
        out_shape=jax.ShapeDtypeStruct((NZ, 2 * ROWS, HDIM), BF),
        in_specs=[vmem()],
        out_specs=vmem(),
        compiler_params=params(),
    )(main)


KEYS = 6144


def cost(rows, keys):
    return pl.CostEstimate(
        flops=rows * keys * HDIM * 8,
        bytes_accessed=2 * keys * HDIM * 2,
        transcendentals=rows * keys,
    )


STATE = jax.ShapeDtypeStruct((NZ * ROWS, HDIM), F32)


def main_own(info, main, text_keys, text_values):
    return pl.pallas_call(
        own_kernel,
        out_shape=(STATE,) * 3,
        in_specs=[smem()] + [vmem()] * 3,
        out_specs=(vmem(),) * 3,
        compiler_params=params(),
        cost_estimate=cost(NZ * ROWS, NZ * ROWS + TXT),
    )(info, main, text_keys, text_values)


def main_near(main, total, state, kv):
    return pl.pallas_call(
        near_kernel,
        out_shape=(STATE,) * 2,
        in_specs=[vmem()] * 5,
        out_specs=(vmem(),) * 2,
        compiler_params=params(),
        cost_estimate=cost(NZ * ROWS, 2 * NZ * ROWS),
    )(main, total, state, *kv)


def main_far(main, total, state, text, kv):
    return pl.pallas_call(
        far_kernel,
        out_shape=jax.ShapeDtypeStruct((NZ, ROWS, HDIM), BF),
        in_specs=[vmem()] * 6,
        out_specs=vmem(),
        compiler_params=params(),
        cost_estimate=cost(NZ * ROWS, NZ * ROWS),
    )(main, total, state, text, *kv)


def shared_attention(kv, columns):
    part = jax.ShapeDtypeStruct((PART_ROWS, HDIM), BF)
    return pl.pallas_call(
        shared_kernel,
        out_shape=(part,) * 4,
        in_specs=[vmem()] * 5,
        out_specs=(vmem(),) * 4,
        compiler_params=params(),
        cost_estimate=cost(NZ * ROWS, NZ * ROWS),
    )(kv, *columns)


def shared_merge(info, queries, parts, text_keys, text_values):
    return pl.pallas_call(
        merge_kernel,
        out_shape=jax.ShapeDtypeStruct((4, ROWS, HDIM), BF),
        in_specs=[smem()] + [vmem()] * 10,
        out_specs=vmem(),
        compiler_params=params(),
        cost_estimate=cost(4 * ROWS, TXT),
    )(info, *queries, *parts, text_keys, text_values)


def head_kernel(
    back_ref, shared_ref, gain_ref, shift_ref, weight_ref, bias_ref, out_ref
):
    blocks = []
    for zl in range(4):
        for zh in range(5):
            start = (5 * zl + zh) * HDIM
            block = back_ref[zh * 4 + zl] if zh < 4 else shared_ref[zl]
            blocks.append((block.astype(F32), slice(start, start + HDIM)))
    count = 20 * HDIM
    average = jnp.sum(sum(block for block, _ in blocks), axis=-1, keepdims=True) / count
    blocks = [(block - average, span) for block, span in blocks]
    variance = sum(block * block for block, _ in blocks)
    variance = jnp.sum(variance, axis=-1, keepdims=True) / count
    scale = lax.rsqrt(variance + 1e-06)
    patches = jnp.zeros((ROWS, 64), F32)
    for block, span in blocks:
        normed = (block * scale * gain_ref[:, span] + shift_ref[:, span]).astype(BF)
        patches = patches + jnp.dot(normed, weight_ref[span, :], preferred_element_type=F32)
    patches = patches + bias_ref[...]
    packed = jnp.concatenate([patches[: ROWS // 2], patches[ROWS // 2 :]], axis=1).astype(BF)
    for copy in range(NZ):
        out_ref[copy] = packed


def head(back, shared, mod_gain, mod_shift, head_weight, head_bias):
    return pl.pallas_call(
        head_kernel,
        out_shape=jax.ShapeDtypeStruct((NZ, ROWS // 2, HDIM), BF),
        in_specs=[vmem()] * 6,
        out_specs=vmem(),
        compiler_params=params(),
    )(back, shared, mod_gain[None], mod_shift[None], head_weight, head_bias[None])


SLAB = 72


def slab_kernel(info, line_ref, out_ref):
    zl = info[3]
    for zh in range(4):
        own = line_ref[zh * 4 + zl].astype(F32)
        above = line_ref[zh * 4 + jnp.maximum(zl - 1, 0)].astype(F32)[PCOL:, 64:]
        below = line_ref[zh * 4 + jnp.minimum(zl + 1, 3)].astype(F32)[:PCOL, :64]
        above = jnp.where(zl > 0, above, 0.0)
        below = jnp.where(zl < 3, below, 0.0)
        left = jnp.concatenate([above, own[:, :64]], axis=0)
        right = jnp.concatenate([own[:, 64:], below], axis=0)
        packed = jnp.concatenate([left, right], axis=1).astype(BF)
        for copy in range(4):
            out_ref[copy, zh] = packed


def slab_of(info, line):
    return pl.pallas_call(
        slab_kernel,
        out_shape=jax.ShapeDtypeStruct((4, 4, SLAB, HDIM), BF),
        in_specs=[smem(), vmem()],
        out_specs=vmem(),
        compiler_params=params(),
    )(info, line)


def conv_kernel(
    info, tile_map, slab_ref, weight_ref, bias_ref, gain_ref, out_ref, wide_ref, pix_ref
):
    wide_ref[...] = jnp.zeros_like(wide_ref)
    for a in range(3):
        for di in (-1, 0, 1):
            for dj in (-1, 0, 1):
                for p in range(2):
                    for q in range(2):
                        row = ((dj + 1) * 4 + p * 2 + q) * LAT
                        for pp in range(2):
                            for qq in range(2):
                                r = 2 * di + p - pp + 1
                                s = 2 * dj + q - qq + 1
                                if 0 <= r < 3 and 0 <= s < 3:
                                    tap = ((a * 3 + r) * 3 + s) * LAT
                                    col = (pp * 2 + qq) * C_OUT
                                    wide_ref[
                                        a * 3 + di + 1, row : row + LAT, col : col + C_OUT
                                    ] = weight_ref[tap : tap + LAT, :]
    x, zh = info[2], info[0]
    pre = jnp.zeros((ROWS, 4 * C_OUT), F32)
    column = lax.broadcasted_iota(jnp.int32, (6 * PCOL, 64), 0) % PCOL
    for a in range(3):
        wanted = 4 * x + zh - 2 + a
        source = jnp.int32(0)
        for b in range(16):
            source = jnp.where(tile_map[b] == wanted, b, source)
        slab = slab_ref[source].astype(F32)
        slab = jnp.concatenate([slab[:, :64], slab[:, 64:]], axis=0)
        slab = jnp.where(wanted >= 0, slab, 0.0)
        zero = jnp.zeros((8, 64), F32)
        tall = jnp.concatenate([zero, slab, zero], axis=0)
        left = jnp.where(column == 0, 0.0, tall[7 : 7 + 6 * PCOL])
        right = jnp.where(column == PCOL - 1, 0.0, tall[9 : 9 + 6 * PCOL])
        joined = jnp.concatenate([left, slab, right], axis=1)
        for di in range(3):
            part = joined[di * PCOL : di * PCOL + ROWS].astype(BF)
            pre = pre + jnp.dot(part, wide_ref[a * 3 + di], preferred_element_type=F32)
    for pp in range(2):
        for qq in range(2):
            at = (pp * 2 + qq) * C_OUT
            value = pre[:, at : at + C_OUT] + bias_ref[...]
            mean = jnp.mean(value * value, axis=-1, keepdims=True)
            value = value * lax.rsqrt(mean + 1e-06) * gain_ref[...]
            value = value / (1.0 + jnp.exp(-value))
            for i in range(4):
                for part in range(3):
                    pix_ref[part, 2 * i + pp, pl.ds(qq, PCOL, 2), :] = value[
                        i * PCOL : (i + 1) * PCOL, part * HDIM : (part + 1) * HDIM
                    ]
    for part in range(3):
        out_ref[:, :, part * HDIM : (part + 1) * HDIM] = pix_ref[part].astype(BF)


def conv(info, tile_map, gathered, conv_weight, conv_bias, norm_gain):
    return pl.pallas_call(
        conv_kernel,
        out_shape=jax.ShapeDtypeStruct((8, 48, C_OUT), BF),
        in_specs=[smem(), smem()] + [vmem()] * 4,
        out_specs=vmem(),
        scratch_shapes=[
            pltpu.VMEM((9, 192, 4 * C_OUT), BF),
            pltpu.VMEM((3, 8, 48, HDIM), F32),
        ],
        compiler_params=params(),
    )(info, tile_map, gathered, conv_weight, conv_bias[None], norm_gain[None])


def shift(block, axis, distance):
    return lax.ppermute(block, axis, [(i, (i + distance) % 4) for i in range(4)])


def around(block, axis):
    right = shift(block, axis, 1)
    left = shift(block, axis, -1)
    half = block.shape[0] // 2
    return (right, left), (shift(right[:half], axis, 1), shift(left[half:], axis, -1))


def exchange(block, axis):
    return lax.all_to_all(block, axis, split_axis=0, concat_axis=0, tiled=True)


def per_device(
    queries,
    keys,
    values,
    text_keys,
    text_values,
    text_len,
    tile_map,
    mod_gain,
    mod_shift,
    head_weight,
    head_bias,
    conv_weight,
    conv_bias,
    norm_gain,
):
    x, zh, zl = (lax.axis_index(axis) for axis in ("x", "zh", "zl"))
    info = jnp.stack([zh, text_len[0], x, zl]).astype(jnp.int32)
    main_send, shared_send, last = load(queries, keys, values)
    last = jnp.stack([last] + [shift(last, "x", d) for d in (1, 2, 3)], axis=1)
    last = [last[0]] + [shift(last[d], "zl", d) for d in (1, 2, 3)]
    main = exchange(main_send, Z)
    main, last, shared_send = lax.optimization_barrier((main, last, shared_send))
    shared = exchange(shared_send, Z)
    near, far = around(key_rows(main), "x")
    total, state, text = main_own(info, main, text_keys, text_values)
    total, state = main_near(main, total, state, near)
    out = main_far(main, total, state, text, far)
    out, shared = lax.optimization_barrier((out, shared))
    back = exchange(out, Z)
    parts = shared_attention(shared, last)
    parts = [parts[0]] + [shift(parts[d], "x", -d) for d in (1, 2, 3)]
    merged = shared_merge(info, last, parts, text_keys, text_values)
    back, merged = lax.optimization_barrier((back, merged))
    shared_back = exchange(merged, "zl")
    line = head(back, shared_back, mod_gain, mod_shift, head_weight, head_bias)
    line = exchange(line, Z)
    plane = exchange(slab_of(info, line), "x")
    gathered = plane.reshape(16, SLAB, HDIM)
    out = conv(info, tile_map, gathered, conv_weight, conv_bias, norm_gain)
    return out[None]


def solution(mesh):
    inner = Mesh(mesh.devices.reshape(8, 4, 4, 4), ("clip", "x", "zh", "zl"))
    tokens = P(("clip", "x", "zh", "zl"), None)
    placed = (
        tokens,
        tokens,
        tokens,
        P("clip", "zl"),
        P("clip", "zl"),
        P("clip"),
        P("clip"),
    ) + (P(),) * 7
    return jax.shard_map(
        per_device,
        mesh=inner,
        in_specs=placed,
        out_specs=P(("clip", "x", "zh"), "zl", None, None),
        check_vma=False,
    )
```

```python
import functools

import jax
import jax.numpy as jnp
from jax import lax
from jax.experimental import pallas as pl
from jax.experimental.pallas import tpu as pltpu
from jax.sharding import Mesh, PartitionSpec as P

PCOL = 24
HDIM = 128
TXT = 512
LAT = 16
ROWS = 96
NZ = 16
C_OUT = 384
LOG2E = 1.4426950408889634
SCALE2 = HDIM ** (-0.5) * LOG2E
Z = ("zh", "zl")
F32 = jnp.float32
BF = jnp.bfloat16
VMEM_LIMIT = 50 * 1024 * 1024


def params():
    return pltpu.CompilerParams(vmem_limit_bytes=VMEM_LIMIT)


def vmem():
    return pl.BlockSpec(memory_space=pltpu.VMEM)


def smem():
    return pl.BlockSpec(memory_space=pltpu.SMEM)


def load_kernel(
    q_hbm, k_hbm, v_hbm, main_out, kv_out, last_out, q_ref, k_ref, v_ref, sems
):
    width = 5 * HDIM
    copies = []
    for zl in range(4):
        span = slice(zl * width, (zl + 1) * width)
        for index, (source, target) in enumerate(((k_hbm, k_ref), (v_hbm, v_ref), (q_hbm, q_ref))):
            copy = pltpu.make_async_copy(
                source.at[:, span], target.at[:, span], sems.at[3 * zl + index]
            )
            copy.start()
            copies.append(copy)
    for zl in range(4):
        for copy in copies[3 * zl : 3 * zl + 3]:
            copy.wait()
        last = slice((5 * zl + 4) * HDIM, (5 * zl + 5) * HDIM)
        for index, ref in enumerate((k_ref, v_ref, q_ref)):
            rows = slice(index * ROWS, (index + 1) * ROWS)
            for zh in range(4):
                own = slice((5 * zl + zh) * HDIM, (5 * zl + zh + 1) * HDIM)
                main_out[zh * 4 + zl, rows, :] = ref[:, own]
                if index < 2:
                    kv_out[zh * 4 + zl, rows, :] = ref[:, last]
    for distance in range(4):
        group = lax.rem(lax.axis_index("zl") + distance, 4)
        span = pl.ds(pl.multiple_of((5 * group + 4) * HDIM, HDIM), HDIM)
        last_out[distance] = q_ref[:, span]


def load(queries, keys, values):
    return pl.pallas_call(
        load_kernel,
        out_shape=(
            jax.ShapeDtypeStruct((NZ, 3 * ROWS, HDIM), BF),
            jax.ShapeDtypeStruct((NZ, 2 * ROWS, HDIM), BF),
            jax.ShapeDtypeStruct((4, ROWS, HDIM), BF),
        ),
        in_specs=[pl.BlockSpec(memory_space=pl.ANY)] * 3,
        out_specs=(vmem(),) * 3,
        scratch_shapes=[pltpu.VMEM((ROWS, 20 * HDIM), BF)] * 3
        + [pltpu.SemaphoreType.DMA((12,))],
        compiler_params=pltpu.CompilerParams(vmem_limit_bytes=60 * 1024 * 1024),
    )(queries, keys, values)


def dot_t(a, b):
    return lax.dot_general(a, b, (((1,), (1,)), ((), ())), preferred_element_type=F32)


def row_peak(scores):
    top = scores[:, :HDIM]
    for col in range(HDIM, scores.shape[1], HDIM):
        top = jnp.maximum(top, scores[:, col : col + HDIM])
    return jnp.max(top, axis=-1, keepdims=True)


def widened(value):
    return jnp.concatenate([value, jnp.ones(value.shape, BF)], axis=1)


def rows_of(piece, first):
    parts = [
        ref[lo:hi, first : first + ROWS, :].reshape((hi - lo) * ROWS, HDIM)
        for ref, lo, hi in piece
    ]
    return parts[0] if len(parts) == 1 else jnp.concatenate(parts, axis=0)


def absorb(groups, pieces, begin, finish):
    steps = [(group, piece) for group in range(len(groups)) for piece in range(len(pieces))]

    def scores_of(step):
        return dot_t(groups[step[0]](), rows_of(pieces[step[1]], 0))

    scores = scores_of(steps[0])
    for index, (group, piece) in enumerate(steps):
        if piece == 0:
            peak, total = begin(group)
        later = scores_of(steps[index + 1]) if index + 1 < len(steps) else None
        highest = row_peak(scores) * SCALE2
        value = widened(rows_of(pieces[piece], ROWS))
        newest = highest if peak is None else jnp.maximum(peak, highest)
        weights = jnp.exp2(scores * SCALE2 - newest).astype(BF)
        part = jnp.dot(weights, value, preferred_element_type=F32)
        total = part if peak is None else total * jnp.exp2(peak - newest) + part
        peak, scores = newest, later
        if piece + 1 == len(pieces):
            finish(group, peak, total)


def fresh(group):
    return None, None


def text_part(query, text_key, text_value, text_len):
    text_scores = dot_t(query, text_key) * SCALE2
    usable = lax.broadcasted_iota(jnp.int32, text_scores.shape, 1) < text_len
    text_scores = jnp.where(usable, text_scores, -1e30)
    text_peak = row_peak(text_scores)
    text_weights = jnp.where(usable, jnp.exp2(text_scores - text_peak), 0.0).astype(BF)
    text_total = jnp.dot(text_weights, widened(text_value), preferred_element_type=F32)
    return text_total[:, :HDIM] / text_total[:, HDIM:]


def pieces_of(refs):
    pieces = []
    for ref in refs:
        for lo in range(0, ref.shape[0], 8):
            part = (ref, lo, min(lo + 8, ref.shape[0]))
            if pieces and sum(hi - lo for _, lo, hi in pieces[-1]) < 8:
                pieces[-1].append(part)
            else:
                pieces.append([part])
    return pieces


GROUP = 4


def rows_in(group):
    return slice(group * GROUP * ROWS, (group + 1) * GROUP * ROWS)


def sources_in(group):
    return slice(group * GROUP, (group + 1) * GROUP)


def queries_of(main_ref):
    def query(group):
        part = main_ref[sources_in(group), 2 * ROWS : 3 * ROWS, :]
        return part.reshape(GROUP * ROWS, HDIM)

    return [functools.partial(query, group) for group in range(NZ // GROUP)]


def state_to(total_ref, state_ref):
    def finish(group, peak, total):
        total_ref[rows_in(group), :] = total[:, :HDIM]
        lane = lax.broadcasted_iota(jnp.int32, (GROUP * ROWS, HDIM), 1)
        state_ref[rows_in(group), :] = jnp.where(lane < 64, peak, total[:, HDIM:])

    return finish


def state_from(total_ref, state_ref):
    def begin(group):
        state = state_ref[rows_in(group), :]
        weight = jnp.broadcast_to(state[:, HDIM - 1 : HDIM], state.shape)
        return state[:, 0:1], jnp.concatenate([total_ref[rows_in(group), :], weight], axis=1)

    return begin


def own_kernel(info, main_ref, tk_ref, tv_ref, total_ref, state_ref, text_ref):
    column = pl.ds(pl.multiple_of(info[0] * HDIM, HDIM), HDIM)
    queries = queries_of(main_ref)
    absorb(queries, pieces_of((main_ref,)), fresh, state_to(total_ref, state_ref))
    for group, query in enumerate(queries):
        text = text_part(query(), tk_ref[:, column], tv_ref[:, column], info[1])
        text_ref[rows_in(group), :] = text


def near_kernel(main_ref, total_in, state_in, k1, k2, total_ref, state_ref):
    begin, finish = state_from(total_in, state_in), state_to(total_ref, state_ref)
    absorb(queries_of(main_ref), pieces_of((k1, k2)), begin, finish)


def far_kernel(main_ref, total_in, state_in, text_in, k3, k4, out_ref):
    def finish(group, peak, total):
        result = total[:, :HDIM] / total[:, HDIM:] + text_in[rows_in(group), :]
        out_ref[sources_in(group)] = result.astype(BF).reshape(GROUP, ROWS, HDIM)

    begin = state_from(total_in, state_in)
    absorb(queries_of(main_ref), pieces_of((k3, k4)), begin, finish)


PART_ROWS = 4 * ROWS + 3 * 16


def shared_kernel(kv_ref, q0, q1, q2, q3, p0, p1, p2, p3):
    rows = 4 * ROWS
    line = lax.broadcasted_iota(jnp.int32, (16, rows), 0)
    outs = (p0, p1, p2, p3)

    def query(column):
        return jnp.concatenate([ref[column] for ref in (q0, q1, q2, q3)], axis=0)

    def finish(column, peak, total):
        outs[column][0:rows] = (total[:, :HDIM] / total[:, HDIM:]).astype(BF)
        level = jnp.transpose(peak + jnp.log2(total[:, HDIM:]))[0:16]
        high = level.astype(BF).astype(F32)
        middle = (level - high).astype(BF).astype(F32)
        low = level - high - middle
        terms = jnp.where(line == 0, high, jnp.where(line == 1, middle, low)).astype(BF)
        for part in range(3):
            start = rows + 16 * part
            outs[column][start : start + 16] = terms[:, part * HDIM : (part + 1) * HDIM]

    queries = [functools.partial(query, column) for column in range(4)]
    absorb(queries, pieces_of((kv_ref,)), fresh, finish)


def level_of(ref):
    columns = []
    for part in range(3):
        start = 4 * ROWS + 16 * part
        terms = ref[start : start + 16].astype(F32)
        level = terms[0:1] + terms[1:2] + terms[2:3]
        columns.append(jnp.transpose(jnp.broadcast_to(level, (HDIM, HDIM))))
    return jnp.concatenate(columns, axis=0)


def merge_kernel(info, q0, q1, q2, q3, p0, p1, p2, p3, tk_ref, tv_ref, out_ref):
    query = jnp.concatenate([ref[0] for ref in (q0, q1, q2, q3)], axis=0)
    parts = (p0, p1, p2, p3)
    levels = [level_of(ref) for ref in parts]
    top = functools.reduce(jnp.maximum, levels)
    weights = [jnp.exp2(level - top) for level in levels]
    result = sum(
        weight * ref[0 : 4 * ROWS].astype(F32) for weight, ref in zip(weights, parts)
    ) / sum(weights)
    column = slice(4 * HDIM, 5 * HDIM)
    result = result + text_part(query, tk_ref[:, column], tv_ref[:, column], info[1])
    for distance in range(4):
        rows = slice(distance * ROWS, (distance + 1) * ROWS)
        out_ref[lax.rem(info[3] + 4 - distance, 4)] = result[rows].astype(BF)


def rows_kernel(main_ref, out_ref):
    out_ref[...] = main_ref[:, 0 : 2 * ROWS, :]


def key_rows(main):
    return pl.pallas_call(
        rows_kernel,
        out_shape=jax.ShapeDtypeStruct((NZ, 2 * ROWS, HDIM), BF),
        in_specs=[vmem()],
        out_specs=vmem(),
        compiler_params=params(),
    )(main)


KEYS = 6144


def cost(rows, keys):
    return pl.CostEstimate(
        flops=rows * keys * HDIM * 8,
        bytes_accessed=2 * keys * HDIM * 2,
        transcendentals=rows * keys,
    )


STATE = jax.ShapeDtypeStruct((NZ * ROWS, HDIM), F32)


def main_own(info, main, text_keys, text_values):
    return pl.pallas_call(
        own_kernel,
        out_shape=(STATE,) * 3,
        in_specs=[smem()] + [vmem()] * 3,
        out_specs=(vmem(),) * 3,
        compiler_params=params(),
        cost_estimate=cost(NZ * ROWS, NZ * ROWS + TXT),
    )(info, main, text_keys, text_values)


def main_near(main, total, state, kv):
    return pl.pallas_call(
        near_kernel,
        out_shape=(STATE,) * 2,
        in_specs=[vmem()] * 5,
        out_specs=(vmem(),) * 2,
        compiler_params=params(),
        cost_estimate=cost(NZ * ROWS, 6 * NZ * ROWS),
    )(main, total, state, *kv)


def main_far(main, total, state, text, kv):
    return pl.pallas_call(
        far_kernel,
        out_shape=jax.ShapeDtypeStruct((NZ, ROWS, HDIM), BF),
        in_specs=[vmem()] * 6,
        out_specs=vmem(),
        compiler_params=params(),
        cost_estimate=cost(NZ * ROWS, 4 * NZ * ROWS),
    )(main, total, state, text, *kv)


def shared_attention(kv, columns):
    part = jax.ShapeDtypeStruct((PART_ROWS, HDIM), BF)
    return pl.pallas_call(
        shared_kernel,
        out_shape=(part,) * 4,
        in_specs=[vmem()] * 5,
        out_specs=(vmem(),) * 4,
        compiler_params=params(),
        cost_estimate=cost(NZ * ROWS, NZ * ROWS),
    )(kv, *columns)


def shared_merge(info, queries, parts, text_keys, text_values):
    return pl.pallas_call(
        merge_kernel,
        out_shape=jax.ShapeDtypeStruct((4, ROWS, HDIM), BF),
        in_specs=[smem()] + [vmem()] * 10,
        out_specs=vmem(),
        compiler_params=params(),
        cost_estimate=cost(4 * ROWS, TXT),
    )(info, *queries, *parts, text_keys, text_values)


def head_kernel(
    back_ref, shared_ref, gain_ref, shift_ref, weight_ref, bias_ref, out_ref
):
    blocks = []
    for zl in range(4):
        for zh in range(5):
            start = (5 * zl + zh) * HDIM
            block = back_ref[zh * 4 + zl] if zh < 4 else shared_ref[zl]
            blocks.append((block.astype(F32), slice(start, start + HDIM)))
    count = 20 * HDIM
    average = jnp.sum(sum(block for block, _ in blocks), axis=-1, keepdims=True) / count
    blocks = [(block - average, span) for block, span in blocks]
    variance = sum(block * block for block, _ in blocks)
    variance = jnp.sum(variance, axis=-1, keepdims=True) / count
    scale = lax.rsqrt(variance + 1e-06)
    patches = jnp.zeros((ROWS, 64), F32)
    for block, span in blocks:
        normed = (block * scale * gain_ref[:, span] + shift_ref[:, span]).astype(BF)
        patches = patches + jnp.dot(normed, weight_ref[span, :], preferred_element_type=F32)
    patches = patches + bias_ref[...]
    packed = jnp.concatenate([patches[: ROWS // 2], patches[ROWS // 2 :]], axis=1).astype(BF)
    for copy in range(NZ):
        out_ref[copy] = packed


def head(back, shared, mod_gain, mod_shift, head_weight, head_bias):
    return pl.pallas_call(
        head_kernel,
        out_shape=jax.ShapeDtypeStruct((NZ, ROWS // 2, HDIM), BF),
        in_specs=[vmem()] * 6,
        out_specs=vmem(),
        compiler_params=params(),
    )(back, shared, mod_gain[None], mod_shift[None], head_weight, head_bias[None])


SLAB = 72


def slab_kernel(info, line_ref, out_ref):
    zl = info[3]
    for zh in range(4):
        own = line_ref[zh * 4 + zl].astype(F32)
        above = line_ref[zh * 4 + jnp.maximum(zl - 1, 0)].astype(F32)[PCOL:, 64:]
        below = line_ref[zh * 4 + jnp.minimum(zl + 1, 3)].astype(F32)[:PCOL, :64]
        above = jnp.where(zl > 0, above, 0.0)
        below = jnp.where(zl < 3, below, 0.0)
        left = jnp.concatenate([above, own[:, :64]], axis=0)
        right = jnp.concatenate([own[:, 64:], below], axis=0)
        packed = jnp.concatenate([left, right], axis=1).astype(BF)
        for copy in range(4):
            out_ref[copy, zh] = packed


def slab_of(info, line):
    return pl.pallas_call(
        slab_kernel,
        out_shape=jax.ShapeDtypeStruct((4, 4, SLAB, HDIM), BF),
        in_specs=[smem(), vmem()],
        out_specs=vmem(),
        compiler_params=params(),
    )(info, line)


def conv_kernel(
    info, tile_map, slab_ref, weight_ref, bias_ref, gain_ref, out_ref, wide_ref, pix_ref
):
    wide_ref[...] = jnp.zeros_like(wide_ref)
    for a in range(3):
        for di in (-1, 0, 1):
            for dj in (-1, 0, 1):
                for p in range(2):
                    for q in range(2):
                        row = ((dj + 1) * 4 + p * 2 + q) * LAT
                        for pp in range(2):
                            for qq in range(2):
                                r = 2 * di + p - pp + 1
                                s = 2 * dj + q - qq + 1
                                if 0 <= r < 3 and 0 <= s < 3:
                                    tap = ((a * 3 + r) * 3 + s) * LAT
                                    col = (pp * 2 + qq) * C_OUT
                                    wide_ref[
                                        a * 3 + di + 1, row : row + LAT, col : col + C_OUT
                                    ] = weight_ref[tap : tap + LAT, :]
    x, zh = info[2], info[0]
    pre = jnp.zeros((ROWS, 4 * C_OUT), F32)
    column = lax.broadcasted_iota(jnp.int32, (6 * PCOL, 64), 0) % PCOL
    for a in range(3):
        wanted = 4 * x + zh - 2 + a
        source = jnp.int32(0)
        for b in range(16):
            source = jnp.where(tile_map[b] == wanted, b, source)
        slab = slab_ref[source].astype(F32)
        slab = jnp.concatenate([slab[:, :64], slab[:, 64:]], axis=0)
        slab = jnp.where(wanted >= 0, slab, 0.0)
        zero = jnp.zeros((8, 64), F32)
        tall = jnp.concatenate([zero, slab, zero], axis=0)
        left = jnp.where(column == 0, 0.0, tall[7 : 7 + 6 * PCOL])
        right = jnp.where(column == PCOL - 1, 0.0, tall[9 : 9 + 6 * PCOL])
        joined = jnp.concatenate([left, slab, right], axis=1)
        for di in range(3):
            part = joined[di * PCOL : di * PCOL + ROWS].astype(BF)
            pre = pre + jnp.dot(part, wide_ref[a * 3 + di], preferred_element_type=F32)
    for pp in range(2):
        for qq in range(2):
            at = (pp * 2 + qq) * C_OUT
            value = pre[:, at : at + C_OUT] + bias_ref[...]
            mean = jnp.mean(value * value, axis=-1, keepdims=True)
            value = value * lax.rsqrt(mean + 1e-06) * gain_ref[...]
            value = value / (1.0 + jnp.exp(-value))
            for i in range(4):
                for part in range(3):
                    pix_ref[part, 2 * i + pp, pl.ds(qq, PCOL, 2), :] = value[
                        i * PCOL : (i + 1) * PCOL, part * HDIM : (part + 1) * HDIM
                    ]
    for part in range(3):
        out_ref[:, :, part * HDIM : (part + 1) * HDIM] = pix_ref[part].astype(BF)


def conv(info, tile_map, gathered, conv_weight, conv_bias, norm_gain):
    return pl.pallas_call(
        conv_kernel,
        out_shape=jax.ShapeDtypeStruct((8, 48, C_OUT), BF),
        in_specs=[smem(), smem()] + [vmem()] * 4,
        out_specs=vmem(),
        scratch_shapes=[
            pltpu.VMEM((9, 192, 4 * C_OUT), BF),
            pltpu.VMEM((3, 8, 48, HDIM), F32),
        ],
        compiler_params=params(),
    )(info, tile_map, gathered, conv_weight, conv_bias[None], norm_gain[None])


def shift(block, axis, distance):
    return lax.ppermute(block, axis, [(i, (i + distance) % 4) for i in range(4)])


def around(block, axis):
    right = shift(block, axis, 1)
    left = shift(block, axis, -1)
    half = block.shape[0] // 2
    return (right, left), (shift(right[:half], axis, 1), shift(left[half:], axis, -1))


def exchange(block, axis):
    return lax.all_to_all(block, axis, split_axis=0, concat_axis=0, tiled=True)


def per_device(
    queries,
    keys,
    values,
    text_keys,
    text_values,
    text_len,
    tile_map,
    mod_gain,
    mod_shift,
    head_weight,
    head_bias,
    conv_weight,
    conv_bias,
    norm_gain,
):
    x, zh, zl = (lax.axis_index(axis) for axis in ("x", "zh", "zl"))
    info = jnp.stack([zh, text_len[0], x, zl]).astype(jnp.int32)
    main_send, shared_send, last = load(queries, keys, values)
    last = jnp.stack([last] + [shift(last, "x", d) for d in (1, 2, 3)], axis=1)
    last = [last[0]] + [shift(last[d], "zl", d) for d in (1, 2, 3)]
    main = exchange(main_send, Z)
    main, last, shared_send = lax.optimization_barrier((main, last, shared_send))
    shared = exchange(shared_send, Z)
    near, far = around(key_rows(main), "x")
    total, state, text = main_own(info, main, text_keys, text_values)
    total, state = main_near(main, total, state, near)
    out = main_far(main, total, state, text, far)
    out, shared = lax.optimization_barrier((out, shared))
    back = exchange(out, Z)
    parts = shared_attention(shared, last)
    parts = [parts[0]] + [shift(parts[d], "x", -d) for d in (1, 2, 3)]
    merged = shared_merge(info, last, parts, text_keys, text_values)
    back, merged = lax.optimization_barrier((back, merged))
    shared_back = exchange(merged, "zl")
    line = head(back, shared_back, mod_gain, mod_shift, head_weight, head_bias)
    line = exchange(line, Z)
    plane = exchange(slab_of(info, line), "x")
    gathered = plane.reshape(16, SLAB, HDIM)
    out = conv(info, tile_map, gathered, conv_weight, conv_bias, norm_gain)
    return out[None]


def solution(mesh):
    inner = Mesh(mesh.devices.reshape(8, 4, 4, 4), ("clip", "x", "zh", "zl"))
    tokens = P(("clip", "x", "zh", "zl"), None)
    placed = (
        tokens,
        tokens,
        tokens,
        P("clip", "zl"),
        P("clip", "zl"),
        P("clip"),
        P("clip"),
    ) + (P(),) * 7
    return jax.shard_map(
        per_device,
        mesh=inner,
        in_specs=placed,
        out_specs=P(("clip", "x", "zh"), "zl", None, None),
        check_vma=False,
    )
```
